512 devices in a mesh: section: 8 (over z_hi, core), dp: 16 (over y, z_lo), mp: 4 (over x).
Axes of the slice: x: 4, y: 4, z: 16 (z_hi: 4, z_lo: 4; z = z_hi * 4 + z_lo), core: 2. Of those that a mesh axis runs over, the one named last changes fastest.
Arguments:
- activations: bfloat16 [8, 4096, 8192], P('section', 'dp', 'mp'), may hold values from -6 to 6
- value_gradient: bfloat16 [8, 4096, 1024], P('section', 'dp', 'mp'), may hold values from -6 to 6
- value_matrix: bfloat16 [8, 8192, 1024], P('section', ('mp', 'dp')), may hold values from -0.1875 to 0.1875
- adapter_down_weight: bfloat16 [8, 16, 32, 8192], P('section', 'dp', None, 'mp'), may hold values from -0.0625 to 0.0625
- adapter_up_weight: bfloat16 [8, 16, 32, 1024], P('section', 'dp', None, 'mp'), may hold values from -0.1875 to 0.1875
- segment_adapter: int32 [8, 32], P('section', 'dp'), may hold values from 0 to 15
- adapter_slot: int32 [16], replicated, may hold values from 0 to 15, each once
Outputs:
- received: bfloat16 [8, 4096, 8192], P('section', 'dp', 'mp')
- down_gradient: bfloat16 [8, 16, 32, 8192], P('section', 'dp', None, 'mp')
- up_gradient: bfloat16 [8, 16, 32, 1024], P('section', 'dp', None, 'mp')
The draws below stay inside these ranges and needn't reach their ends.
Inputs may be any that keep to these rules, and one draw needn't show every extreme that they name: adapter_slot is a permutation of the adapters.
All inputs are finite; a program needn't handle non-finite values.
Results may differ from the reference program's by a relative error of at most 0.025.
Values may be sent and summed in bfloat16 or wider, within the bound.
A program may use at most 64 MiB of HBM per device.

```python
import math
import jax
import jax.numpy as jnp
import numpy as np
from jax import lax

MODEL_WIDTH = 8192
VALUE_WIDTH = 1024
ADAPTER_RANK = 32
RELAY_SECTIONS = 8
SECTION_TOKENS = 4096
SEGMENTS = 32
ADAPTER_TOTAL = 16
N_DP = 16


def set_ends(drawn, key, smallest, largest):
    longest = drawn.shape.index(max(drawn.shape))
    spots = []
    for shift in (0, 1):
        where = [jax.random.randint(jax.random.fold_in(key, axis), (), 0, length) for axis, length in enumerate(drawn.shape)]
        where[longest] = (where[longest] + shift) % drawn.shape[longest]
        spots.append(tuple(where))
    return drawn.at[spots[0]].set(smallest).at[spots[1]].set(largest)


def block_scale(stream_key, shape, split, low, largest):
    def one(axis_at, blocks):
        heights = jax.random.uniform(jax.random.fold_in(jax.random.fold_in(stream_key, 6), axis_at), (blocks,), jnp.float32, low / len(split), largest / len(split))
        return jnp.repeat(jnp.exp(heights), shape[axis_at] // blocks).reshape((-1,) + (1,) * (len(shape) - axis_at - 1))

    level = one(*split[0])
    for cut in split[1:]:
        level = level * one(*cut)
    return level


def cumulative_ranks(number_of, skew):
    loads = [(1 << 20) // math.isqrt(standing ** skew) + 1 for standing in range(1, number_of + 1)]
    width = 1 + sum(loads) // (1 << 30)
    return np.cumsum(np.array([max(1, weight // width) for weight in loads]))


def skewed_ids(key, shape, count, lean):
    grid = cumulative_ranks(count, lean)
    ticket = jax.random.randint(jax.random.fold_in(key, 1), shape, 0, int(grid[count - 1]))
    grade = jnp.searchsorted(jnp.asarray(grid, jnp.int32), ticket, side="right")
    return jax.random.permutation(jax.random.fold_in(key, 2), count)[grade].astype(jnp.int32)


def scatter_about(key, shape, width, most, shards=(), held_as=jnp.bfloat16):
    values = jax.random.normal(key, shape, jnp.float32) * width
    if len(shards) > 0:
        values = block_scale(key, shape, shards, -0.22, 0.18) * values
    return jnp.clip(values, min=-most, max=most).astype(held_as)


def setup_inputs(seed: int = 0) -> dict:
    arg_keys = jax.random.split(jax.random.key(seed), 8)
    return {
        "activations": scatter_about(arg_keys[0], (RELAY_SECTIONS, SECTION_TOKENS, MODEL_WIDTH), 1.0, 6.0, ((0, 8), (1, 16), (2, 4))),
        "value_gradient": scatter_about(arg_keys[1], (RELAY_SECTIONS, SECTION_TOKENS, VALUE_WIDTH), 1.0, 6.0, ((0, 8), (1, 16), (2, 4))),
        "value_matrix": scatter_about(arg_keys[2], (RELAY_SECTIONS, MODEL_WIDTH, VALUE_WIDTH), VALUE_WIDTH ** -0.5, 0.1875, ((0, 8), (1, 64))),
        "adapter_down_weight": scatter_about(arg_keys[3], (RELAY_SECTIONS, ADAPTER_TOTAL, ADAPTER_RANK, MODEL_WIDTH), MODEL_WIDTH ** -0.5, 0.0625, ((0, 8), (1, 16), (3, 4))),
        "adapter_up_weight": scatter_about(arg_keys[4], (RELAY_SECTIONS, ADAPTER_TOTAL, ADAPTER_RANK, VALUE_WIDTH), VALUE_WIDTH ** -0.5, 0.1875, ((0, 8), (1, 16), (3, 4))),
        "segment_adapter": set_ends(skewed_ids(arg_keys[5], (RELAY_SECTIONS, SEGMENTS), ADAPTER_TOTAL, 2), jax.random.fold_in(arg_keys[5], 3), 0, ADAPTER_TOTAL - 1).astype(jnp.int32),
        "adapter_slot": jax.random.permutation(arg_keys[6], ADAPTER_TOTAL).astype(jnp.int32),
    }


ADAPTER_SCALE = 2.0

def rounded(value):
    return lax.optimization_barrier(value.astype(jnp.bfloat16)).astype(jnp.float32)

def single_section(kernel_arguments, adapter_slot):
    activations, value_gradient, value_matrix, adapter_down_weight, adapter_up_weight, segment_adapter = kernel_arguments
    adapter_number = adapter_down_weight.shape[0]
    segment_count = segment_adapter.shape[0]
    complete_width = activations.shape[1]
    value_width = value_gradient.shape[1]
    slot_position = jnp.take(adapter_slot, segment_adapter).astype(jnp.int32)
    picked = (slot_position[:, None] == jnp.arange(adapter_number, dtype=jnp.int32)[None, :]).astype(jnp.float32)
    down_segment = jnp.take(adapter_down_weight, slot_position, axis=0).astype(jnp.float32)
    up_segment = jnp.take(adapter_up_weight, slot_position, axis=0).astype(jnp.float32)
    token_seg = activations.reshape(segment_count, -1, complete_width).astype(jnp.float32)
    grad_seg = value_gradient.reshape(segment_count, -1, value_width).astype(jnp.float32)
    hidden = rounded(jnp.einsum('ksd,krd->ksr', token_seg, down_segment))
    rank_gradient = rounded(jnp.einsum('ksv,krv->ksr', grad_seg, up_segment))
    frozen_term = jnp.dot(value_gradient, value_matrix.T, preferred_element_type=jnp.float32)
    adapter_term = jnp.einsum('xcf,xfv->xcv', rank_gradient, down_segment).reshape(-1, complete_width)
    input_gradient = (frozen_term + ADAPTER_SCALE * adapter_term).astype(jnp.bfloat16)
    gradient_norm = ADAPTER_SCALE / math.sqrt(SECTION_TOKENS / ADAPTER_TOTAL)
    part_down = jnp.einsum('ksr,ksd->krd', rank_gradient, token_seg)
    partial_up = jnp.einsum('ksr,ksv->krv', hidden, grad_seg)
    per_dev = segment_count // N_DP
    pick_dev = picked.reshape(N_DP, per_dev, adapter_number)
    dev_down = jnp.einsum('ika,ikrd->iard', pick_dev, part_down.reshape(N_DP, per_dev, ADAPTER_RANK, complete_width), precision=lax.Precision.HIGHEST) * gradient_norm
    dev_up = jnp.einsum('ika,ikrv->iarv', pick_dev, partial_up.reshape(N_DP, per_dev, ADAPTER_RANK, value_width), precision=lax.Precision.HIGHEST) * gradient_norm
    down_gradient = lax.optimization_barrier(jnp.sum(rounded(dev_down), axis=0)).astype(jnp.bfloat16)
    up_gradient = lax.optimization_barrier(jnp.sum(rounded(dev_up), axis=0)).astype(jnp.bfloat16)
    return (input_gradient, down_gradient, up_gradient)

def reference(activations, value_gradient, value_matrix, adapter_down_weight, adapter_up_weight, segment_adapter, adapter_slot):
    input_gradient, down_gradient, up_gradient = lax.map(lambda kernel_arguments: single_section(kernel_arguments, adapter_slot), (activations, value_gradient, value_matrix, adapter_down_weight, adapter_up_weight, segment_adapter))
    received = jnp.roll(input_gradient, -1, axis=0)
    return (received, down_gradient, up_gradient)
```

```python
import functools
import math

import jax
import jax.numpy as jnp
from jax import lax
from jax.experimental import pallas as pl
from jax.experimental.pallas import tpu as pltpu
from jax.sharding import PartitionSpec as P

ADAPTERS_PER_DP = 1
ADAPTER_SCALE = 2.0
MESH = pl.DeviceIdType.MESH
BF16 = jnp.bfloat16
F32 = jnp.float32

NY = 4
NZ = 4
NX = 4
NS = 8


def nt_dot(a, b):
    return lax.dot_general(a, b, (((1,), (1,)), ((), ())), preferred_element_type=F32)


def nn_dot(a, b):
    return lax.dot_general(a, b, (((1,), (0,)), ((), ())), preferred_element_type=F32)


def tn_dot(a, b):
    return lax.dot_general(a, b, (((0,), (0,)), ((), ())), preferred_element_type=F32)


def kernel(
    act, grad, wmat, down, up, seg, slot,
    out, dgrad, ugrad,
    wn, gf, dns, dn, si, sin, uz, usel, ur, dz, dsel, dr,
    pm, rp, rr, rt, rtn, rx, hp, ht, pd, st, rsd, pu, su, rsu, ot,
    shift_s, w_r, w_s, g_r, g_sy, g_sx, dns_r, dna_r, dna_s, dnz_r, dnz_s,
    si_r, si_s, sin_r, sin_s, uz_r, uz_s, ur_r, ur_s, dz_r, dz_s, dr_r, dr_s,
    rp_r, rp_s, rtn_r, rtn_s, hp_r, hp_s, pd_r, pd_s, rsd_r, rsd_s,
    pu_r, pu_s, rsu_r, rsu_s, o_r, o_s,
):
    s = lax.axis_index("section")
    d = lax.axis_index("dp")
    x = lax.axis_index("mp")
    y, z = d // NZ, d % NZ
    first_core = s % 2 == 0
    before, after = (s + NS - 1) % NS, (s + 1) % NS
    rows = act.shape[0]
    seg_rows = rows // 2
    rank = down.shape[0]
    norm = ADAPTER_SCALE / math.sqrt(rows / ADAPTERS_PER_DP)

    def at(s_=s, y_=y, z_=z, x_=x):
        return {"section": s_, "dp": y_ * NZ + z_, "mp": x_}

    def copy(src, dst, ss, rs, device):
        return pltpu.make_async_remote_copy(
            src_ref=src, dst_ref=dst, send_sem=ss, recv_sem=rs,
            device_id=device, device_id_type=MESH,
        )

    def send(src, dst, ss, rs, device):
        copy(src, dst, ss, rs, device).start()

    def arrived(dst, rs):
        copy(dst, dst, rs, rs, at()).wait_recv()

    def sent(src, ss):
        copy(src, src, ss, ss, at()).wait_send()

    y_peers = [(y + k) % NY for k in (1, 3, 2)]
    x_peers = [(x + k) % NX for k in (1, 3, 2)]
    z_peers = [(z + k) % NZ for k in (1, 2, 3)]

    bar = pltpu.get_barrier_semaphore()
    peers = (
        [at(y_=p) for p in y_peers] + [at(x_=p) for p in x_peers] + [at(z_=p) for p in z_peers]
        + [at(s_=before, y_=k) for k in range(NY)] + [at(s_=after, y_=k) for k in range(NY)]
    )
    for p in peers:
        pl.semaphore_signal(bar, inc=1, device_id=p, device_id_type=MESH)
    pl.semaphore_wait(bar, len(peers))

    def line_out(buf, i, ss, rs, right, left):
        @pl.when(jnp.logical_and(right, z < NZ - 1))
        def _():
            send(buf.at[i], buf.at[i], ss.at[0, i], rs.at[i], at(z_=z + 1))

        @pl.when(jnp.logical_and(left, z > 0))
        def _():
            send(buf.at[i], buf.at[i], ss.at[1, i], rs.at[i], at(z_=z - 1))

    def line_step(buf, t, ss, rs):
        lo, hi = z - t, z + t

        @pl.when(lo >= 0)
        def _():
            arrived(buf.at[lo], rs.at[lo])
            line_out(buf, lo, ss, rs, True, False)

        @pl.when(hi < NZ)
        def _():
            arrived(buf.at[hi], rs.at[hi])
            line_out(buf, hi, ss, rs, False, True)

    def line_sent(buf, ss):
        for i in range(NZ):
            @pl.when(jnp.logical_and(i <= z, z < NZ - 1))
            def _():
                sent(buf.at[i], ss.at[0, i])

            @pl.when(jnp.logical_and(i >= z, z > 0))
            def _():
                sent(buf.at[i], ss.at[1, i])

    si[y, 0:1, :] = jnp.full((1, 128), slot[seg[0]], jnp.int32)
    si[y, 1:2, :] = jnp.full((1, 128), slot[seg[1]], jnp.int32)
    for k, p in enumerate(y_peers):
        send(si.at[y], si.at[y], si_s.at[k], si_r.at[y], at(y_=p))
    for k in range(NY):
        send(si.at[y], sin.at[y], sin_s.at[k], sin_r.at[y], at(s_=before, y_=k))
    uz[z] = up[...]
    line_out(uz, z, uz_s, uz_r, True, True)
    g_here = gf.at[x, pl.ds(pl.multiple_of(y * rows, rows), rows)]
    send(grad, g_here, shift_s.at[0], g_r.at[x, y], at(s_=before))
    send(wmat, wn.at[z], shift_s.at[1], w_r.at[z], at(s_=before))
    send(down, dns, shift_s.at[2], dns_r, at(s_=before))
    dz[z] = down[...]
    line_out(dz, z, dz_s, dz_r, True, True)

    def start_next():
        arrived(g_here, g_r.at[x, y])
        for k, p in enumerate(x_peers):
            send(g_here, g_here, g_sx.at[k, y], g_r.at[x, y], at(x_=p))
        for k, p in enumerate(y_peers):
            send(g_here, g_here, g_sy.at[k], g_r.at[x, y], at(y_=p))
        arrived(wn.at[z], w_r.at[z])
        line_out(wn, z, w_s, w_r, True, True)
        arrived(dns, dns_r)
        width = dn.shape[2]
        for k, p in enumerate(y_peers):
            cols = pl.ds(pl.multiple_of(p * width, width), width)
            mine = pl.ds(pl.multiple_of(y * rank, rank), rank)
            send(dns.at[:, cols], dn.at[z, mine], dna_s.at[k], dna_r.at[y], at(y_=p))
        own = pl.ds(pl.multiple_of(y * width, width), width)
        dn[z, pl.ds(pl.multiple_of(y * rank, rank), rank), :] = dns[:, own]

    @pl.when(first_core)
    def _():
        start_next()

    for p in y_peers:
        arrived(si.at[p], si_r.at[p])
    col = lax.broadcasted_iota(jnp.int32, (rank, 128), 1)
    row = lax.broadcasted_iota(jnp.int32, (rank, 128), 0)
    same = row == col % rank
    here = y * NZ + col // rank
    for p in range(NY):
        for k in range(2):
            ids = jnp.broadcast_to(si[p, k:k + 1, :], (rank, 128))
            hit = jnp.where(jnp.logical_and(ids == here, same), 1.0, 0.0)
            pm[pl.ds((p * 2 + k) * rank, rank), :] = hit.astype(BF16)

    for t in range(1, NZ):
        line_step(uz, t, uz_s, uz_r)
    usel[...] = nn_dot(pm[...], uz[...].reshape(NZ * rank, up.shape[1])).astype(BF16)
    mine64 = pl.ds(pl.multiple_of(y * 2 * rank, 2 * rank), 2 * rank)

    def rows_of(p):
        return pl.ds(pl.multiple_of(p * 2 * rank, 2 * rank), 2 * rank)

    for k, p in enumerate(y_peers):
        send(usel.at[rows_of(p)], ur.at[y], ur_s.at[k], ur_r.at[y], at(y_=p))
    ur[y] = usel[mine64, :]

    for t in range(1, NZ):
        line_step(dz, t, dz_s, dz_r)
    for j in range(4):
        c = slice(j * 512, (j + 1) * 512)
        dsel[:, c] = nn_dot(pm[...], dz[:, :, c].reshape(NZ * rank, 512)).astype(BF16)
    for k, p in enumerate(y_peers):
        send(dsel.at[rows_of(p)], dr.at[y], dr_s.at[k], dr_r.at[y], at(y_=p))
    dr[y] = dsel[mine64, :]

    for p in y_peers:
        arrived(ur.at[p], ur_r.at[p])
    picked = sum(ur[p].astype(F32) for p in range(NY)).astype(BF16)
    for k in range(2):
        lanes = slice(k * seg_rows, (k + 1) * seg_rows)
        rp[x, :, lanes] = nt_dot(picked[k * rank:(k + 1) * rank], grad[lanes, :])
    for k, p in enumerate(x_peers):
        send(rp.at[x], rp.at[x], rp_s.at[k], rp_r.at[x], at(x_=p))
    for p in x_peers:
        arrived(rp.at[p], rp_r.at[p])
    rt[...] = sum(rp[p] for p in range(NX)).astype(BF16)
    for k in range(NY):
        send(rt, rtn.at[y], rtn_s.at[k], rtn_r.at[y], at(s_=before, y_=k))
    for k in range(2):
        lanes = slice(k * seg_rows, (k + 1) * seg_rows)
        part = nn_dot(rt[:, lanes], act[lanes, :]) * norm
        pd[y, k * rank:(k + 1) * rank, :] = part.astype(BF16)
    for k, p in enumerate(y_peers):
        send(pd.at[y], pd.at[y], pd_s.at[k], pd_r.at[y], at(y_=p))

    for p in y_peers:
        arrived(dr.at[p], dr_r.at[p])
    for k in range(2):
        lanes = slice(k * seg_rows, (k + 1) * seg_rows)
        r32 = slice(k * rank, (k + 1) * rank)
        picked = sum(dr[p, r32, :].astype(F32) for p in range(NY)).astype(BF16)
        hp[x, :, lanes] = nt_dot(picked, act[lanes, :])
    for k, p in enumerate(x_peers):
        send(hp.at[x], hp.at[x], hp_s.at[k], hp_r.at[x], at(x_=p))

    for p in y_peers:
        arrived(pd.at[p], pd_r.at[p])
    for j in range(4):
        c = slice(j * 512, (j + 1) * 512)
        st[:, c] = tn_dot(pm[...], pd[:, :, c].reshape(NY * 2 * rank, 512)).astype(BF16)

    def rank_rows(p):
        return pl.ds(pl.multiple_of(p * rank, rank), rank)

    for k, p in enumerate(z_peers):
        send(st.at[rank_rows(p)], rsd.at[z], rsd_s.at[k], rsd_r.at[z], at(z_=p))
    rsd[z] = st[rank_rows(z), :]

    for p in x_peers:
        arrived(hp.at[p], hp_r.at[p])
    ht[...] = sum(hp[p] for p in range(NX)).astype(BF16)
    for k in range(2):
        lanes = slice(k * seg_rows, (k + 1) * seg_rows)
        part = nn_dot(ht[:, lanes], grad[lanes, :]) * norm
        pu[y, k * rank:(k + 1) * rank, :] = part.astype(BF16)
    for k, p in enumerate(y_peers):
        send(pu.at[y], pu.at[y], pu_s.at[k], pu_r.at[y], at(y_=p))

    @pl.when(jnp.logical_not(first_core))
    def _():
        start_next()

    for p in y_peers:
        arrived(pu.at[p], pu_r.at[p])
    su[...] = tn_dot(pm[...], pu[...].reshape(NY * 2 * rank, up.shape[1])).astype(BF16)
    for k, p in enumerate(z_peers):
        send(su.at[rank_rows(p)], rsu.at[z], rsu_s.at[k], rsu_r.at[z], at(z_=p))
    rsu[z] = su[rank_rows(z), :]

    def g_block(x_, y_):
        return gf.at[x_, pl.ds(pl.multiple_of(y_ * rows, rows), rows)]

    for p in y_peers:
        arrived(g_block(x, p), g_r.at[x, p])
        for k, q in enumerate(x_peers):
            send(g_block(x, p), g_block(x, p), g_sx.at[k, p], g_r.at[x, p], at(x_=q))
    for p in y_peers:
        arrived(dn.at[z, rank_rows(p)], dna_r.at[p])
    line_out(dn, z, dnz_s, dnz_r, True, True)

    spread = jnp.where(
        lax.broadcasted_iota(jnp.int32, (rank, rx.shape[1]), 0)
        == lax.broadcasted_iota(jnp.int32, (rank, rx.shape[1]), 1) % rank,
        ADAPTER_SCALE, 0.0,
    ).astype(BF16)
    cols = lax.broadcasted_iota(jnp.int32, (seg_rows, rx.shape[1]), 1)
    col_slot = (cols // rank) % NY * NZ + cols // (rank * NY)
    for p in range(NY):
        arrived(sin.at[p], sin_r.at[p])
        arrived(rtn.at[p], rtn_r.at[p])
        for k in range(2):
            wide = tn_dot(rtn[p, :, k * seg_rows:(k + 1) * seg_rows], spread)
            ids = jnp.broadcast_to(sin[p, k:k + 1, 0:1], wide.shape)
            rx[pl.ds(p * rows + k * seg_rows, seg_rows), :] = jnp.where(
                ids == col_slot, wide, 0.0
            ).astype(BF16)
    for t in range(1, NZ):
        line_step(dn, t, dnz_s, dnz_r)
    for q in x_peers:
        for p in range(NY):
            arrived(g_block(q, p), g_r.at[q, p])

    chunk = wmat.shape[0]

    def compute(i):
        lanes = pl.ds(pl.multiple_of(i * chunk, chunk), chunk)
        place = pl.ds(pl.multiple_of(y * (NZ * chunk) + i * chunk, chunk), chunk)
        for p in range(NY):
            r = slice(p * rows, (p + 1) * rows)
            total = nn_dot(rx[r, :], dn[:, :, lanes].reshape(rx.shape[1], chunk))
            for q in range(NX):
                total += nt_dot(gf[q, r, :], wn[i, :, q * rows:(q + 1) * rows])
            ot[i, r, :] = total.astype(BF16)
        for k, p in enumerate(y_peers):
            r = pl.ds(pl.multiple_of(p * rows, rows), rows)
            send(ot.at[i, r], out.at[:, place], o_s.at[k, i], o_r.at[y, i], at(y_=p))
        out[:, place] = ot[i, pl.ds(pl.multiple_of(y * rows, rows), rows), :]

    compute(z)

    @pl.loop(1, NZ)
    def _(t):
        lo, hi = z - t, z + t

        @pl.when(lo >= 0)
        def _():
            arrived(wn.at[lo], w_r.at[lo])
            line_out(wn, lo, w_s, w_r, True, False)

        @pl.when(hi < NZ)
        def _():
            arrived(wn.at[hi], w_r.at[hi])
            line_out(wn, hi, w_s, w_r, False, True)

        @pl.when(lo >= 0)
        def _():
            compute(lo)

        @pl.when(hi < NZ)
        def _():
            compute(hi)

    for p in z_peers:
        arrived(rsd.at[p], rsd_r.at[p])
    dgrad[...] = sum(rsd[p].astype(F32) for p in range(NZ)).astype(BF16)
    for p in z_peers:
        arrived(rsu.at[p], rsu_r.at[p])
    ugrad[...] = sum(rsu[p].astype(F32) for p in range(NZ)).astype(BF16)

    for p in y_peers:
        for i in range(NZ):
            place = pl.ds(pl.multiple_of((p * NZ + i) * chunk, chunk), chunk)
            arrived(out.at[:, place], o_r.at[p, i])
    sent(grad, shift_s.at[0])
    sent(wmat, shift_s.at[1])
    sent(down, shift_s.at[2])
    line_sent(uz, uz_s)
    line_sent(dz, dz_s)
    line_sent(dn, dnz_s)
    line_sent(wn, w_s)
    for k in range(NY):
        sent(si.at[0], sin_s.at[k])
        sent(rt, rtn_s.at[k])
    for k in range(3):
        sent(si.at[0], si_s.at[k])
        sent(g_here, g_sy.at[k])
        for p in range(NY):
            sent(g_here, g_sx.at[k, p])
        sent(dn.at[0, pl.ds(0, rank)], dna_s.at[k])
        sent(ur.at[0], ur_s.at[k])
        sent(dr.at[0], dr_s.at[k])
        sent(rp.at[0], rp_s.at[k])
        sent(hp.at[0], hp_s.at[k])
        sent(pd.at[0], pd_s.at[k])
        sent(pu.at[0], pu_s.at[k])
        sent(rsd.at[0], rsd_s.at[k])
        sent(rsu.at[0], rsu_s.at[k])
        for i in range(NZ):
            sent(ot.at[0, pl.ds(0, rows)], o_s.at[k, i])


def body(
    activations,
    value_gradient,
    value_matrix,
    adapter_down_weight,
    adapter_up_weight,
    segment_adapter,
    adapter_slot,
):
    rows, width = activations.shape[1:]
    values = value_gradient.shape[2]
    w_rows, v_width = value_matrix.shape[1:]
    rank = adapter_down_weight.shape[2]
    slots = adapter_slot.shape[0]
    piece = width // NY
    vmem = pl.BlockSpec(memory_space=pltpu.VMEM)
    smem = pl.BlockSpec(memory_space=pltpu.SMEM)
    dma = lambda *shape: pltpu.SemaphoreType.DMA(shape)
    scratch = [
        pltpu.VMEM((NZ, w_rows, v_width), BF16),
        pltpu.VMEM((NX, NY * rows, values), BF16),
        pltpu.VMEM((rank, width), BF16),
        pltpu.VMEM((NZ, NY * rank, piece), BF16),
        pltpu.VMEM((NY, 8, 128), jnp.int32),
        pltpu.VMEM((NY, 8, 128), jnp.int32),
        pltpu.VMEM((NZ, rank, values), BF16),
        pltpu.VMEM((NY * 2 * rank, values), BF16),
        pltpu.VMEM((NY, 2 * rank, values), BF16),
        pltpu.VMEM((NZ, rank, width), BF16),
        pltpu.VMEM((NY * 2 * rank, width), BF16),
        pltpu.VMEM((NY, 2 * rank, width), BF16),
        pltpu.VMEM((NY * 2 * rank, NZ * rank), BF16),
        pltpu.VMEM((NX, rank, rows), F32),
        pltpu.VMEM((8, 128), F32),
        pltpu.VMEM((rank, rows), BF16),
        pltpu.VMEM((NY, rank, rows), BF16),
        pltpu.VMEM((NY * rows, slots * rank), BF16),
        pltpu.VMEM((NX, rank, rows), F32),
        pltpu.VMEM((rank, rows), BF16),
        pltpu.VMEM((NY, 2 * rank, width), BF16),
        pltpu.VMEM((NZ * rank, width), BF16),
        pltpu.VMEM((NZ, rank, width), BF16),
        pltpu.VMEM((NY, 2 * rank, values), BF16),
        pltpu.VMEM((NZ * rank, values), BF16),
        pltpu.VMEM((NZ, rank, values), BF16),
        pltpu.VMEM((NZ, NY * rows, w_rows), BF16),
        dma(3), dma(NZ), dma(2, NZ), dma(NX, NY), dma(3), dma(3, NY),
        pltpu.SemaphoreType.DMA, dma(NY), dma(3), dma(NZ), dma(2, NZ),
        dma(NY), dma(3), dma(NY), dma(NY),
        dma(NZ), dma(2, NZ), dma(NY), dma(3),
        dma(NZ), dma(2, NZ), dma(NY), dma(3),
        dma(NX), dma(3), dma(NY), dma(NY),
        dma(NX), dma(3), dma(NY), dma(3), dma(NZ), dma(3),
        dma(NY), dma(3), dma(NZ), dma(3),
        dma(NY, NZ), dma(3, NZ),
    ]
    received, down_gradient, up_gradient = pl.pallas_call(
        kernel,
        out_shape=(
            jax.ShapeDtypeStruct((rows, width), BF16),
            jax.ShapeDtypeStruct((rank, width), BF16),
            jax.ShapeDtypeStruct((rank, values), BF16),
        ),
        in_specs=[vmem] * 5 + [smem] * 2,
        out_specs=(vmem, vmem, vmem),
        scratch_shapes=scratch,
        compiler_params=pltpu.CompilerParams(
            collective_id=0, has_side_effects=True, vmem_limit_bytes=48 << 20
        ),
        name="relay_backward",
    )(
        activations[0],
        value_gradient[0],
        value_matrix[0],
        adapter_down_weight[0, 0],
        adapter_up_weight[0, 0],
        segment_adapter[0],
        adapter_slot,
    )
    return received[None], down_gradient[None, None], up_gradient[None, None]


def solution(mesh):
    placed = (
        P("section", "dp", "mp"),
        P("section", "dp", "mp"),
        P("section", ("mp", "dp"), None),
        P("section", "dp", None, "mp"),
        P("section", "dp", None, "mp"),
        P("section", "dp"),
        P(),
    )
    return jax.shard_map(
        body,
        mesh=mesh,
        in_specs=placed,
        out_specs=(
            P("section", "dp", "mp"),
            P("section", "dp", None, "mp"),
            P("section", "dp", None, "mp"),
        ),
        check_vma=False,
    )
```

```python
import functools
import math

import jax
import jax.numpy as jnp
from jax import lax
from jax.experimental import pallas as pl
from jax.experimental.pallas import tpu as pltpu
from jax.sharding import PartitionSpec as P

ADAPTERS_PER_DP = 1
ADAPTER_SCALE = 2.0
MESH = pl.DeviceIdType.MESH
BF16 = jnp.bfloat16
F32 = jnp.float32

NY = 4
NZ = 4
NX = 4
NS = 8
NP = 2


def nt_dot(a, b):
    return lax.dot_general(a, b, (((1,), (1,)), ((), ())), preferred_element_type=F32)


def nn_dot(a, b):
    return lax.dot_general(a, b, (((1,), (0,)), ((), ())), preferred_element_type=F32)


def tn_dot(a, b):
    return lax.dot_general(a, b, (((0,), (0,)), ((), ())), preferred_element_type=F32)


def kernel(
    act_hbm, grad_hbm, wmat, down, up, seg, slot,
    out, dgrad, ugrad,
    act, grad, wn, gf, dns, dn, si, sin, uz, usel, ur, dz, dsel, dr,
    pm, rp, rt, rtn, rx, hp, ht, pd, st, rsd, pu, su, rsu, ot,
    local_s, shift_s, w_r, w_s, g_r, g_sy, g_sx, dns_r, dna_r, dna_s, dnz_r, dnz_s,
    si_r, si_s, sin_r, sin_s, uz_r, uz_s, ur_r, ur_s, dz_r, dz_s, dr_r, dr_s,
    rp_r, rp_s, rtn_r, rtn_s, hp_r, hp_s, pd_r, pd_s, rsd_r, rsd_s,
    pu_r, pu_s, rsu_r, rsu_s, o_r, o_s,
):
    s = lax.axis_index("section")
    d = lax.axis_index("dp")
    x = lax.axis_index("mp")
    y, z = d // NZ, d % NZ
    before, after = (s + NS - 1) % NS, (s + 1) % NS
    rows = act.shape[0]
    seg_rows = rows // 2
    rank = down.shape[0]
    piece = dn.shape[2]
    chunk = wmat.shape[0]
    wp = chunk // NP
    norm = ADAPTER_SCALE / math.sqrt(rows / ADAPTERS_PER_DP)

    def at(s_=s, y_=y, z_=z, x_=x):
        return {"section": s_, "dp": y_ * NZ + z_, "mp": x_}

    def copy(src, dst, ss, rs, device):
        return pltpu.make_async_remote_copy(
            src_ref=src, dst_ref=dst, send_sem=ss, recv_sem=rs,
            device_id=device, device_id_type=MESH,
        )

    def arrived(dst, rs):
        copy(dst, dst, rs, rs, at()).wait_recv()

    def sent(src, ss):
        copy(src, src, ss, ss, at()).wait_send()

    def block(i, n):
        return pl.ds(i * n, n) if isinstance(i, int) else pl.ds(pl.multiple_of(i * n, n), n)

    y_peers = [(y + k) % NY for k in (1, 3, 2)]
    x_peers = [(x + k) % NX for k in (1, 3, 2)]
    z_peers = [(z + k) % NZ for k in (1, 2, 3)]
    segments = [slice(k * seg_rows, (k + 1) * seg_rows) for k in range(2)]
    ranks = [slice(k * rank, (k + 1) * rank) for k in range(2)]
    wide = 2 * rank
    columns = [slice(j, j + 512) for j in range(0, act.shape[1], 512)]
    who = [None]
    started = []

    def send(like, src, dst, ss, rs, device, when=None):
        started.append((who[0], when, like, ss))

        def start():
            copy(src, dst, ss[0].at[ss[1:]], rs, device).start()

        if when is None:
            start()
        else:
            pl.when(when())(start)

    def on(core, *steps):
        who[0] = core

        def run():
            for step in steps:
                step()

        if core is None:
            run()
        else:
            pl.when(s % 2 == core)(run)
        who[0] = None

    loads = [
        pltpu.make_async_copy(src, dst, local_s.at[k])
        for k, (src, dst) in enumerate(
            [(up, uz.at[z]), (grad_hbm, grad), (down, dz.at[z]), (act_hbm, act)]
        )
    ]
    for load in loads:
        load.start()

    bar = pltpu.get_barrier_semaphore()
    peers = (
        [at(y_=p) for p in y_peers] + [at(x_=p) for p in x_peers] + [at(z_=p) for p in z_peers]
        + [at(s_=before, y_=k) for k in range(NY)] + [at(s_=after, y_=k) for k in range(NY)]
    )
    for p in peers:
        pl.semaphore_signal(bar, inc=1, device_id=p, device_id_type=MESH)
    si[y, 0:1, :] = jnp.full((1, 128), slot[seg[0]], jnp.int32)
    si[y, 1:2, :] = jnp.full((1, 128), slot[seg[1]], jnp.int32)
    pl.semaphore_wait(bar, len(peers))

    def g_block(x_, y_):
        return gf.at[x_, block(y_, rows)]

    def w_piece(i, p):
        return wn.at[i, p * wp:(p + 1) * wp]

    def slots_out():
        for k, p in enumerate(y_peers):
            send(lambda: si.at[0], si.at[y], si.at[y], (si_s, k), si_r.at[y], at(y_=p))

    def up_out():
        for k, p in enumerate(z_peers):
            send(up, up, uz.at[z], (uz_s, k), uz_r.at[z], at(z_=p))

    def down_out():
        for k, p in enumerate(z_peers):
            send(down, down, dz.at[z], (dz_s, k), dz_r.at[z], at(z_=p))

    def slots_next_out():
        for k in range(NY):
            send(lambda: si.at[0], si.at[y], sin.at[y], (sin_s, k), sin_r.at[y], at(s_=before, y_=k))

    def w_shift():
        for p in range(NP):
            send(lambda p=p: w_piece(0, p), wmat.at[p * wp:(p + 1) * wp], w_piece(z, p), (shift_s, p), w_r.at[z, p], at(s_=before))

    def g_shift():
        send(grad, grad_hbm, g_block(x, y), (shift_s, NP), g_r.at[x, y], at(s_=before))

    def down_shift():
        send(dns, down, dns, (shift_s, NP + 1), dns_r, at(s_=before))

    def g_start_y():
        arrived(g_block(x, y), g_r.at[x, y])
        for k, p in enumerate(y_peers):
            send(grad, g_block(x, y), g_block(x, y), (g_sy, k), g_r.at[x, y], at(y_=p))

    def g_start_x():
        for k, p in enumerate(x_peers):
            send(grad, g_block(x, y), g_block(x, y), (g_sx, k, 0), g_r.at[x, y], at(x_=p))

    def g_relay():
        for j, p in enumerate(y_peers):
            arrived(g_block(x, p), g_r.at[x, p])
            for k, q in enumerate(x_peers):
                send(grad, g_block(x, p), g_block(x, p), (g_sx, k, 1 + j), g_r.at[x, p], at(x_=q))

    def w_out(t, p, way):
        i, z_to = (z - t, z + 1) if way == 0 else (z + t, z - 1)

        def when():
            if way == 0:
                return jnp.logical_and(z < NZ - 1, z >= t)
            return jnp.logical_and(z > 0, z < NZ - t)

        send(lambda p=p: w_piece(0, p), w_piece(i, p), w_piece(i, p), (w_s, way, t, p), w_r.at[i, p], at(z_=z_to), when)

    def w_start():
        for p in range(NP):
            arrived(w_piece(z, p), w_r.at[z, p])
            w_out(0, p, 1)
            w_out(0, p, 0)

    def w_step(t):
        lo, hi = z - t, z + t
        for p in range(NP):
            pl.when(hi < NZ)(functools.partial(arrived, w_piece(hi, p), w_r.at[hi, p]))
            w_out(t, p, 1)
            pl.when(lo >= 0)(functools.partial(arrived, w_piece(lo, p), w_r.at[lo, p]))
            w_out(t, p, 0)

    def picks():
        for p in y_peers:
            arrived(si.at[p], si_r.at[p])
        col = lax.broadcasted_iota(jnp.int32, (rank, 128), 1)
        row = lax.broadcasted_iota(jnp.int32, (rank, 128), 0)
        same = row == col % rank
        here = y * NZ + col // rank
        for p in range(NY):
            for k in range(2):
                ids = jnp.broadcast_to(si[p, k:k + 1, :], (rank, 128))
                hit = jnp.where(jnp.logical_and(ids == here, same), 1.0, 0.0)
                pm[pl.ds((p * 2 + k) * rank, rank), :] = hit.astype(BF16)

    def up_pick():
        loads[0].wait()
        for p in z_peers:
            arrived(uz.at[p], uz_r.at[p])
        usel[...] = nn_dot(pm[...], uz[...].reshape(NZ * rank, up.shape[1])).astype(BF16)
        for k, p in enumerate(y_peers):
            send(lambda: ur.at[0], usel.at[block(p, wide)], ur.at[y], (ur_s, k), ur_r.at[y], at(y_=p))
        ur[y] = usel[block(y, wide), :]

    def rank_part():
        loads[1].wait()
        for p in y_peers:
            arrived(ur.at[p], ur_r.at[p])
        picked = sum(ur[p].astype(F32) for p in range(NY)).astype(BF16)
        for r, lanes in zip(ranks, segments):
            rp[x, :, lanes] = nt_dot(picked[r], grad[lanes, :])
        for k, p in enumerate(x_peers):
            send(lambda: rp.at[0], rp.at[x], rp.at[x], (rp_s, k), rp_r.at[x], at(x_=p))

    def rank_sum():
        for p in x_peers:
            arrived(rp.at[p], rp_r.at[p])
        rt[...] = sum(rp[p] for p in range(NX)).astype(BF16)
        for k in range(NY):
            send(rt, rt, rtn.at[y], (rtn_s, k), rtn_r.at[y], at(s_=before, y_=k))

    def down_part():
        loads[3].wait()
        for r, lanes in zip(ranks, segments):
            pd[y, r, :] = (nn_dot(rt[:, lanes], act[lanes, :]) * norm).astype(BF16)
        for k, p in enumerate(y_peers):
            send(lambda: pd.at[0], pd.at[y], pd.at[y], (pd_s, k), pd_r.at[y], at(y_=p))

    def down_sum():
        for p in y_peers:
            arrived(pd.at[p], pd_r.at[p])
        for c in columns:
            st[:, c] = tn_dot(pm[...], pd[:, :, c].reshape(NY * wide, 512)).astype(BF16)
        for k, p in enumerate(z_peers):
            send(lambda: rsd.at[0], st.at[block(p, rank)], rsd.at[z], (rsd_s, k), rsd_r.at[z], at(z_=p))
        rsd[z] = st[block(z, rank), :]

    def down_end():
        for p in z_peers:
            arrived(rsd.at[p], rsd_r.at[p])
        dgrad[...] = sum(rsd[p].astype(F32) for p in range(NZ)).astype(BF16)

    def down_wait():
        loads[2].wait()
        for p in z_peers:
            arrived(dz.at[p], dz_r.at[p])

    def down_next():
        for k in range(NY):
            send(lambda: dn.at[:, block(0, rank)], dz.at[:, :, block(k, piece)], dn.at[:, block(y, rank)],
                 (dna_s, k), dna_r.at[y], at(s_=before, y_=k))

    def down_pick():
        for c in columns:
            dsel[:, c] = nn_dot(pm[...], dz[:, :, c].reshape(NZ * rank, 512)).astype(BF16)
        for k, p in enumerate(y_peers):
            send(lambda: dr.at[0], dsel.at[block(p, wide)], dr.at[y], (dr_s, k), dr_r.at[y], at(y_=p))
        dr[y] = dsel[block(y, wide), :]

    def hidden_part():
        for p in y_peers:
            arrived(dr.at[p], dr_r.at[p])
        for r, lanes in zip(ranks, segments):
            picked = sum(dr[p, r, :].astype(F32) for p in range(NY)).astype(BF16)
            hp[x, :, lanes] = nt_dot(picked, act[lanes, :])
        for k, p in enumerate(x_peers):
            send(lambda: hp.at[0], hp.at[x], hp.at[x], (hp_s, k), hp_r.at[x], at(x_=p))

    def up_part():
        for p in x_peers:
            arrived(hp.at[p], hp_r.at[p])
        ht[...] = sum(hp[p] for p in range(NX)).astype(BF16)
        for r, lanes in zip(ranks, segments):
            pu[y, r, :] = (nn_dot(ht[:, lanes], grad[lanes, :]) * norm).astype(BF16)
        for k, p in enumerate(y_peers):
            send(lambda: pu.at[0], pu.at[y], pu.at[y], (pu_s, k), pu_r.at[y], at(y_=p))

    def up_sum():
        for p in y_peers:
            arrived(pu.at[p], pu_r.at[p])
        su[...] = tn_dot(pm[...], pu[...].reshape(NY * wide, up.shape[1])).astype(BF16)
        for k, p in enumerate(z_peers):
            send(lambda: rsu.at[0], su.at[block(p, rank)], rsu.at[z], (rsu_s, k), rsu_r.at[z], at(z_=p))
        rsu[z] = su[block(z, rank), :]

    def up_end():
        for p in z_peers:
            arrived(rsu.at[p], rsu_r.at[p])
        ugrad[...] = sum(rsu[p].astype(F32) for p in range(NZ)).astype(BF16)

    def dn_start():
        arrived(dns, dns_r)
        for k, p in enumerate(y_peers):
            send(lambda: dn.at[0, block(0, rank)], dns.at[:, block(p, piece)], dn.at[z, block(y, rank)],
                 (dna_s, NY + k), dna_r.at[y], at(y_=p))
        dn[z, block(y, rank), :] = dns[:, block(y, piece)]

    def dn_relay():
        for p in y_peers:
            arrived(dn.at[z, block(p, rank)], dna_r.at[p])
        for k, p in enumerate(z_peers):
            send(lambda: dn.at[0], dn.at[z], dn.at[z], (dnz_s, k), dnz_r.at[z], at(z_=p))

    def dn_wait0():
        for p in range(NY):
            arrived(dn.at[:, block(p, rank)], dna_r.at[p])

    def dn_wait1():
        for p in z_peers:
            arrived(dn.at[p], dnz_r.at[p])

    slots_wide = rx.shape[1]

    def rank_spread():
        spread = jnp.where(
            lax.broadcasted_iota(jnp.int32, (rank, slots_wide), 0)
            == lax.broadcasted_iota(jnp.int32, (rank, slots_wide), 1) % rank,
            ADAPTER_SCALE, 0.0,
        ).astype(BF16)
        cols = lax.broadcasted_iota(jnp.int32, (seg_rows, slots_wide), 1)
        col_slot = (cols // rank) % NY * NZ + cols // (rank * NY)
        for p in range(NY):
            arrived(sin.at[p], sin_r.at[p])
            arrived(rtn.at[p], rtn_r.at[p])
            for k, lanes in enumerate(segments):
                spread_out = tn_dot(rtn[p, :, lanes], spread)
                ids = jnp.broadcast_to(sin[p, k:k + 1, 0:1], spread_out.shape)
                rx[pl.ds(p * rows + k * seg_rows, seg_rows), :] = jnp.where(
                    ids == col_slot, spread_out, 0.0
                ).astype(BF16)

    def g_wait():
        for q in x_peers:
            for p in range(NY):
                arrived(g_block(q, p), g_r.at[q, p])

    def product(i):
        place = block(y * NZ + i, chunk)
        for p in range(NY):
            r = slice(p * rows, (p + 1) * rows)
            total = nn_dot(rx[r, :], dn[:, :, block(i, chunk)].reshape(slots_wide, chunk))
            for q in range(NX):
                total += nt_dot(gf[q, r, :], wn[i, :, q * rows:(q + 1) * rows])
            ot[i, r, :] = total.astype(BF16)
        for k, p in enumerate(y_peers):
            copy(ot.at[i, block(p, rows)], out.at[:, place], o_s.at[k, i], o_r.at[y, i], at(y_=p)).start()
        out[:, place] = ot[i, block(y, rows), :]

    def products():
        @pl.loop(0, NZ)
        def _(t):
            for side, i in enumerate((z - t, z + t)):
                @pl.when(i >= 0 if side == 0 else jnp.logical_and(i < NZ, t > 0))
                def _():
                    @pl.when(t == NZ - 1)
                    def _():
                        for p in range(NP):
                            arrived(w_piece(i, p), w_r.at[i, p])
                    product(i)

        for i in range(NZ):
            for k in range(3):
                started.append((who[0], None, lambda: ot.at[0, block(0, rows)], (o_s, k, i)))

    def out_end():
        for p in y_peers:
            for i in range(NZ):
                arrived(out.at[:, block(p * NZ + i, chunk)], o_r.at[p, i])

    def w_step1():
        w_step(1)

    def w_step2():
        w_step(2)

    on(None, slots_out, up_out, w_shift, g_shift)
    on(0, down_shift)
    on(None, down_out, slots_next_out)
    on(0, w_start, g_start_y, g_start_x)
    on(None, picks, up_pick)
    on(0, g_relay)
    on(None, rank_part, rank_sum, down_part)
    on(0, w_step1)
    on(None, rank_spread)
    on(1, w_start, g_start_y, g_start_x, dn_start)
    on(None, down_wait)
    on(1, down_next)
    on(None, down_pick)
    on(0, w_step2)
    on(1, w_step1, g_relay, dn_relay)
    on(None, down_sum)
    on(1, w_step2)
    on(None, hidden_part)
    on(0, dn_wait0, g_wait, products)
    on(None, up_part)
    on(1, dn_wait1, g_wait, products)
    on(None, up_sum, down_end, up_end, out_end)

    for core in (None, 0, 1):
        group = [e[1:] for e in started if e[0] == core]

        def finish():
            for when, like, ss in group:
                def wait():
                    sent(like() if callable(like) else like, ss[0].at[ss[1:]])

                if when is None:
                    wait()
                else:
                    pl.when(when())(wait)

        on(core, finish)


def body(
    activations,
    value_gradient,
    value_matrix,
    adapter_down_weight,
    adapter_up_weight,
    segment_adapter,
    adapter_slot,
):
    rows, width = activations.shape[1:]
    values = value_gradient.shape[2]
    w_rows, v_width = value_matrix.shape[1:]
    rank = adapter_down_weight.shape[2]
    slots = adapter_slot.shape[0]
    piece = width // NY
    vmem = pl.BlockSpec(memory_space=pltpu.VMEM)
    hbm = pl.BlockSpec(memory_space=pltpu.HBM)
    smem = pl.BlockSpec(memory_space=pltpu.SMEM)
    dma = lambda *shape: pltpu.SemaphoreType.DMA(shape)
    scratch = [
        pltpu.VMEM((rows, width), BF16),
        pltpu.VMEM((rows, values), BF16),
        pltpu.VMEM((NZ, w_rows, v_width), BF16),
        pltpu.VMEM((NX, NY * rows, values), BF16),
        pltpu.VMEM((rank, width), BF16),
        pltpu.VMEM((NZ, NY * rank, piece), BF16),
        pltpu.VMEM((NY, 8, 128), jnp.int32),
        pltpu.VMEM((NY, 8, 128), jnp.int32),
        pltpu.VMEM((NZ, rank, values), BF16),
        pltpu.VMEM((NY * 2 * rank, values), BF16),
        pltpu.VMEM((NY, 2 * rank, values), BF16),
        pltpu.VMEM((NZ, rank, width), BF16),
        pltpu.VMEM((NY * 2 * rank, width), BF16),
        pltpu.VMEM((NY, 2 * rank, width), BF16),
        pltpu.VMEM((NY * 2 * rank, NZ * rank), BF16),
        pltpu.VMEM((NX, rank, rows), F32),
        pltpu.VMEM((rank, rows), BF16),
        pltpu.VMEM((NY, rank, rows), BF16),
        pltpu.VMEM((NY * rows, slots * rank), BF16),
        pltpu.VMEM((NX, rank, rows), F32),
        pltpu.VMEM((rank, rows), BF16),
        pltpu.VMEM((NY, 2 * rank, width), BF16),
        pltpu.VMEM((NZ * rank, width), BF16),
        pltpu.VMEM((NZ, rank, width), BF16),
        pltpu.VMEM((NY, 2 * rank, values), BF16),
        pltpu.VMEM((NZ * rank, values), BF16),
        pltpu.VMEM((NZ, rank, values), BF16),
        pltpu.VMEM((NZ, NY * rows, w_rows), BF16),
        dma(4), dma(NP + 2), dma(NZ, NP), dma(2, NZ, NP),
        dma(NX, NY), dma(3), dma(3, NY),
        pltpu.SemaphoreType.DMA, dma(NY), dma(NY + 3), dma(NZ), dma(3),
        dma(NY), dma(3), dma(NY), dma(NY),
        dma(NZ), dma(3), dma(NY), dma(3),
        dma(NZ), dma(3), dma(NY), dma(3),
        dma(NX), dma(3), dma(NY), dma(NY),
        dma(NX), dma(3), dma(NY), dma(3), dma(NZ), dma(3),
        dma(NY), dma(3), dma(NZ), dma(3),
        dma(NY, NZ), dma(3, NZ),
    ]
    received, down_gradient, up_gradient = pl.pallas_call(
        kernel,
        out_shape=(
            jax.ShapeDtypeStruct((rows, width), BF16),
            jax.ShapeDtypeStruct((rank, width), BF16),
            jax.ShapeDtypeStruct((rank, values), BF16),
        ),
        in_specs=[hbm] * 5 + [smem] * 2,
        out_specs=(vmem, vmem, vmem),
        scratch_shapes=scratch,
        compiler_params=pltpu.CompilerParams(
            collective_id=0, has_side_effects=True, vmem_limit_bytes=63 << 20
        ),
        name="relay_backward",
    )(
        activations[0],
        value_gradient[0],
        value_matrix[0],
        adapter_down_weight[0, 0],
        adapter_up_weight[0, 0],
        segment_adapter[0],
        adapter_slot,
    )
    return received[None], down_gradient[None, None], up_gradient[None, None]


def solution(mesh):
    placed = (
        P("section", "dp", "mp"),
        P("section", "dp", "mp"),
        P("section", ("mp", "dp"), None),
        P("section", "dp", None, "mp"),
        P("section", "dp", None, "mp"),
        P("section", "dp"),
        P(),
    )
    return jax.shard_map(
        body,
        mesh=mesh,
        in_specs=placed,
        out_specs=(
            P("section", "dp", "mp"),
            P("section", "dp", None, "mp"),
            P("section", "dp", None, "mp"),
        ),
        check_vma=False,
    )
```

```python
import functools
import math

import jax
import jax.numpy as jnp
from jax import lax
from jax.experimental import pallas as pl
from jax.experimental.pallas import tpu as pltpu
from jax.sharding import PartitionSpec as P

ADAPTERS_PER_DP = 1
ADAPTER_SCALE = 2.0
MESH = pl.DeviceIdType.MESH
BF16 = jnp.bfloat16
F32 = jnp.float32

NY = 4
NZ = 4
NX = 4
NS = 8
NP = 2


def nt_dot(a, b):
    return lax.dot_general(a, b, (((1,), (1,)), ((), ())), preferred_element_type=F32)


def nn_dot(a, b):
    return lax.dot_general(a, b, (((1,), (0,)), ((), ())), preferred_element_type=F32)


def tn_dot(a, b):
    return lax.dot_general(a, b, (((0,), (0,)), ((), ())), preferred_element_type=F32)


def kernel(
    act_hbm, grad_hbm, wmat, down, up, seg, slot,
    out, dgrad, ugrad,
    act, grad, wn, gf, dns, far, dn, si, sin, uz, usel, ur, dz, dsel, dr,
    pm, rp, rt, rtn, rx, hp, ht, pd, st, rsd, pu, su, rsu, ot,
    local_s, shift_s, w_r, w_s, g_r, g_sy, g_sx, far_r, far_s, dns_r, dna_r, dna_s, dnz_r, dnz_s,
    si_r, si_s, sin_r, sin_s, uz_r, uz_s, ur_r, ur_s, dz_r, dz_s, dr_r, dr_s,
    rp_r, rp_s, rtn_r, rtn_s, hp_r, hp_s, pd_r, pd_s, rsd_r, rsd_s,
    pu_r, pu_s, rsu_r, rsu_s, o_r, o_s,
):
    s = lax.axis_index("section")
    d = lax.axis_index("dp")
    x = lax.axis_index("mp")
    y, z = d // NZ, d % NZ
    before, after = (s + NS - 1) % NS, (s + 1) % NS
    rows = act.shape[0]
    seg_rows = rows // 2
    rank = down.shape[0]
    piece = dn.shape[2]
    chunk = wmat.shape[0]
    wp = chunk // NP
    norm = ADAPTER_SCALE / math.sqrt(rows / ADAPTERS_PER_DP)

    def at(s_=s, y_=y, z_=z, x_=x):
        return {"section": s_, "dp": y_ * NZ + z_, "mp": x_}

    def copy(src, dst, ss, rs, device):
        return pltpu.make_async_remote_copy(
            src_ref=src, dst_ref=dst, send_sem=ss, recv_sem=rs,
            device_id=device, device_id_type=MESH,
        )

    def arrived(dst, rs):
        copy(dst, dst, rs, rs, at()).wait_recv()

    def sent(src, ss):
        copy(src, src, ss, ss, at()).wait_send()

    def block(i, n):
        return pl.ds(i * n, n) if isinstance(i, int) else pl.ds(pl.multiple_of(i * n, n), n)

    y_peers = [(y + k) % NY for k in (1, 3, 2)]
    x_peers = [(x + k) % NX for k in (1, 3, 2)]
    z_peers = [(z + k) % NZ for k in (1, 2, 3)]
    segments = [slice(k * seg_rows, (k + 1) * seg_rows) for k in range(2)]
    ranks = [slice(k * rank, (k + 1) * rank) for k in range(2)]
    wide = 2 * rank
    columns = [slice(j, j + 512) for j in range(0, act.shape[1], 512)]
    who = [None]
    started = []

    def send(like, src, dst, ss, rs, device, when=None):
        started.append((who[0], when, like, ss))

        def start():
            copy(src, dst, ss[0].at[ss[1:]], rs, device).start()

        if when is None:
            start()
        else:
            pl.when(when())(start)

    def on(core, *steps):
        who[0] = core

        def run():
            for step in steps:
                step()

        if core is None:
            run()
        else:
            pl.when(s % 2 == core)(run)
        who[0] = None

    loads = [
        pltpu.make_async_copy(src, dst, local_s.at[k])
        for k, (src, dst) in enumerate(
            [(up, uz.at[z]), (grad_hbm, grad), (down, dz.at[z]), (act_hbm, act)]
        )
    ]
    for load in loads:
        load.start()

    bar = pltpu.get_barrier_semaphore()
    peers = (
        [at(y_=p) for p in y_peers] + [at(x_=p) for p in x_peers] + [at(z_=p) for p in z_peers]
        + [at(s_=before, y_=k) for k in range(NY)] + [at(s_=after, y_=k) for k in range(NY)]
        + [at(s_=(s + 2) % NS), at(s_=(s + 6) % NS), at(s_=(s + 3 + 2 * (s % 2)) % NS)]
    )
    for p in peers:
        pl.semaphore_signal(bar, inc=1, device_id=p, device_id_type=MESH)
    si[y, 0:1, :] = jnp.full((1, 128), slot[seg[0]], jnp.int32)
    si[y, 1:2, :] = jnp.full((1, 128), slot[seg[1]], jnp.int32)
    pl.semaphore_wait(bar, len(peers))

    def g_block(x_, y_):
        return gf.at[x_, block(y_, rows)]

    def w_piece(i, p):
        return wn.at[i, p * wp:(p + 1) * wp]

    def slots_out():
        for k, p in enumerate(y_peers):
            send(lambda: si.at[0], si.at[y], si.at[y], (si_s, k), si_r.at[y], at(y_=p))

    def up_out():
        for k, p in enumerate(z_peers):
            send(up, up, uz.at[z], (uz_s, k), uz_r.at[z], at(z_=p))

    def down_out():
        for k, p in enumerate(z_peers):
            send(down, down, dz.at[z], (dz_s, k), dz_r.at[z], at(z_=p))

    def slots_next_out():
        for k in range(NY):
            send(lambda: si.at[0], si.at[y], sin.at[y], (sin_s, k), sin_r.at[y], at(s_=before, y_=k))

    def w_shift():
        for p in range(NP):
            send(lambda p=p: w_piece(0, p), wmat.at[p * wp:(p + 1) * wp], w_piece(z, p), (shift_s, p), w_r.at[z, p], at(s_=before))

    def g_shift():
        send(grad, grad_hbm, g_block(x, y), (shift_s, NP), g_r.at[x, y], at(s_=before))

    def far0():
        send(down, down, far.at[0], (far_s, 0), far_r.at[0], at(s_=(s + 2) % NS))

    def far1():
        arrived(far.at[0], far_r.at[0])
        send(dns, far.at[0], far.at[1], (far_s, 1), far_r.at[1], at(s_=(s + 2) % NS))

    def far2():
        arrived(far.at[1], far_r.at[1])
        send(dns, far.at[1], dns, (far_s, 2), dns_r, at(s_=(s + 3) % NS))

    def g_start_y():
        arrived(g_block(x, y), g_r.at[x, y])
        for k, p in enumerate(y_peers):
            send(grad, g_block(x, y), g_block(x, y), (g_sy, k), g_r.at[x, y], at(y_=p))

    def g_start_x():
        for k, p in enumerate(x_peers):
            send(grad, g_block(x, y), g_block(x, y), (g_sx, k, 0), g_r.at[x, y], at(x_=p))

    def g_relay():
        for j, p in enumerate(y_peers):
            arrived(g_block(x, p), g_r.at[x, p])
            for k, q in enumerate(x_peers):
                send(grad, g_block(x, p), g_block(x, p), (g_sx, k, 1 + j), g_r.at[x, p], at(x_=q))

    def w_out(t, p, way):
        i, z_to = (z - t, z + 1) if way == 0 else (z + t, z - 1)

        def when():
            if way == 0:
                return jnp.logical_and(z < NZ - 1, z >= t)
            return jnp.logical_and(z > 0, z < NZ - t)

        send(lambda p=p: w_piece(0, p), w_piece(i, p), w_piece(i, p), (w_s, way, t, p), w_r.at[i, p], at(z_=z_to), when)

    def w_start():
        for p in range(NP):
            arrived(w_piece(z, p), w_r.at[z, p])
            w_out(0, p, 1)
            w_out(0, p, 0)

    def w_step(t):
        lo, hi = z - t, z + t
        for p in range(NP):
            pl.when(hi < NZ)(functools.partial(arrived, w_piece(hi, p), w_r.at[hi, p]))
            w_out(t, p, 1)
            pl.when(lo >= 0)(functools.partial(arrived, w_piece(lo, p), w_r.at[lo, p]))
            w_out(t, p, 0)

    def picks():
        for p in y_peers:
            arrived(si.at[p], si_r.at[p])
        col = lax.broadcasted_iota(jnp.int32, (rank, 128), 1)
        row = lax.broadcasted_iota(jnp.int32, (rank, 128), 0)
        same = row == col % rank
        here = y * NZ + col // rank
        for p in range(NY):
            for k in range(2):
                ids = jnp.broadcast_to(si[p, k:k + 1, :], (rank, 128))
                hit = jnp.where(jnp.logical_and(ids == here, same), 1.0, 0.0)
                pm[pl.ds((p * 2 + k) * rank, rank), :] = hit.astype(BF16)

    def up_pick():
        loads[0].wait()
        for p in z_peers:
            arrived(uz.at[p], uz_r.at[p])
        usel[...] = nn_dot(pm[...], uz[...].reshape(NZ * rank, up.shape[1])).astype(BF16)
        for k, p in enumerate(y_peers):
            send(lambda: ur.at[0], usel.at[block(p, wide)], ur.at[y], (ur_s, k), ur_r.at[y], at(y_=p))
        ur[y] = usel[block(y, wide), :]

    def rank_part():
        loads[1].wait()
        for p in y_peers:
            arrived(ur.at[p], ur_r.at[p])
        picked = sum(ur[p].astype(F32) for p in range(NY)).astype(BF16)
        for r, lanes in zip(ranks, segments):
            rp[x, :, lanes] = nt_dot(picked[r], grad[lanes, :])
        for k, p in enumerate(x_peers):
            send(lambda: rp.at[0], rp.at[x], rp.at[x], (rp_s, k), rp_r.at[x], at(x_=p))

    def rank_sum():
        for p in x_peers:
            arrived(rp.at[p], rp_r.at[p])
        rt[...] = sum(rp[p] for p in range(NX)).astype(BF16)
        for k in range(NY):
            send(rt, rt, rtn.at[y], (rtn_s, k), rtn_r.at[y], at(s_=before, y_=k))

    def down_part():
        loads[3].wait()
        for r, lanes in zip(ranks, segments):
            pd[y, r, :] = (nn_dot(rt[:, lanes], act[lanes, :]) * norm).astype(BF16)
        for k, p in enumerate(y_peers):
            send(lambda: pd.at[0], pd.at[y], pd.at[y], (pd_s, k), pd_r.at[y], at(y_=p))

    def down_way(way, q, when):
        z_to = z - 1 if way == 0 else z + 1
        send(lambda: rsd.at[0, 0], rsd.at[way, q], rsd.at[way, q], (rsd_s, way, q), rsd_r.at[way, q], at(z_=z_to), when)

    def down_sum():
        for p in y_peers:
            arrived(pd.at[p], pd_r.at[p])
        for c in columns:
            st[:, :, c] = tn_dot(pm[...], pd[:, :, c].reshape(NY * wide, 512)).astype(BF16).reshape(NZ, rank, 512)

        @pl.when(z == NZ - 1)
        def _():
            for q in range(NZ - 1):
                rsd[0, q] = st[q]

        @pl.when(z == 0)
        def _():
            for q in range(1, NZ):
                rsd[1, q] = st[q]

        for q in range(NZ - 1):
            down_way(0, q, lambda: z == NZ - 1)
        for q in range(NZ - 1, 0, -1):
            down_way(1, q, lambda: z == 0)

    def down_hop(way, q, here):
        @pl.when(z == here)
        def _():
            arrived(rsd.at[way, q], rsd_r.at[way, q])
            rsd[way, q] = (rsd[way, q].astype(F32) + st[q].astype(F32)).astype(BF16)

        down_way(way, q, lambda: z == here)

    def down_hop1():
        for k in range(2):
            down_hop(0, k, 2)
            down_hop(1, 3 - k, 1)

    def down_hop2():
        down_hop(0, 0, 1)
        down_hop(1, 3, 2)

    def down_end():
        pl.when(z < NZ - 1)(lambda: arrived(rsd.at[0, z], rsd_r.at[0, z]))
        pl.when(z > 0)(lambda: arrived(rsd.at[1, z], rsd_r.at[1, z]))
        total = st[z].astype(F32)
        total += jnp.where(z < NZ - 1, rsd[0, z].astype(F32), 0.0)
        total += jnp.where(z > 0, rsd[1, z].astype(F32), 0.0)
        dgrad[...] = total.astype(BF16)

    def down_wait():
        loads[2].wait()
        for p in z_peers:
            arrived(dz.at[p], dz_r.at[p])

    def down_next():
        for k in range(NY):
            send(lambda: dn.at[:, block(0, rank)], dz.at[:, :, block(k, piece)], dn.at[:, block(y, rank)],
                 (dna_s, k), dna_r.at[y], at(s_=before, y_=k))

    def down_pick():
        for c in columns:
            dsel[:, c] = nn_dot(pm[...], dz[:, :, c].reshape(NZ * rank, 512)).astype(BF16)
        for k, p in enumerate(y_peers):
            send(lambda: dr.at[0], dsel.at[block(p, wide)], dr.at[y], (dr_s, k), dr_r.at[y], at(y_=p))
        dr[y] = dsel[block(y, wide), :]

    def hidden_part():
        for p in y_peers:
            arrived(dr.at[p], dr_r.at[p])
        for r, lanes in zip(ranks, segments):
            picked = sum(dr[p, r, :].astype(F32) for p in range(NY)).astype(BF16)
            hp[x, :, lanes] = nt_dot(picked, act[lanes, :])
        for k, p in enumerate(x_peers):
            send(lambda: hp.at[0], hp.at[x], hp.at[x], (hp_s, k), hp_r.at[x], at(x_=p))

    def up_part():
        for p in x_peers:
            arrived(hp.at[p], hp_r.at[p])
        ht[...] = sum(hp[p] for p in range(NX)).astype(BF16)
        for r, lanes in zip(ranks, segments):
            pu[y, r, :] = (nn_dot(ht[:, lanes], grad[lanes, :]) * norm).astype(BF16)
        for k, p in enumerate(y_peers):
            send(lambda: pu.at[0], pu.at[y], pu.at[y], (pu_s, k), pu_r.at[y], at(y_=p))

    def up_sum():
        for p in y_peers:
            arrived(pu.at[p], pu_r.at[p])
        su[...] = tn_dot(pm[...], pu[...].reshape(NY * wide, up.shape[1])).astype(BF16)
        for k, p in enumerate(z_peers):
            send(lambda: rsu.at[0], su.at[block(p, rank)], rsu.at[z], (rsu_s, k), rsu_r.at[z], at(z_=p))
        rsu[z] = su[block(z, rank), :]

    def up_end():
        for p in z_peers:
            arrived(rsu.at[p], rsu_r.at[p])
        ugrad[...] = sum(rsu[p].astype(F32) for p in range(NZ)).astype(BF16)

    def dn_start():
        arrived(dns, dns_r)
        for k, p in enumerate(y_peers):
            send(lambda: dn.at[0, block(0, rank)], dns.at[:, block(p, piece)], dn.at[z, block(y, rank)],
                 (dna_s, NY + k), dna_r.at[y], at(y_=p))
        dn[z, block(y, rank), :] = dns[:, block(y, piece)]

    def dn_relay():
        for p in y_peers:
            arrived(dn.at[z, block(p, rank)], dna_r.at[p])
        for k, p in enumerate(z_peers):
            send(lambda: dn.at[0], dn.at[z], dn.at[z], (dnz_s, k), dnz_r.at[z], at(z_=p))

    def dn_wait0():
        for p in range(NY):
            arrived(dn.at[:, block(p, rank)], dna_r.at[p])

    def dn_wait1():
        for p in z_peers:
            arrived(dn.at[p], dnz_r.at[p])

    slots_wide = rx.shape[1]

    def rank_spread():
        spread = jnp.where(
            lax.broadcasted_iota(jnp.int32, (rank, slots_wide), 0)
            == lax.broadcasted_iota(jnp.int32, (rank, slots_wide), 1) % rank,
            ADAPTER_SCALE, 0.0,
        ).astype(BF16)
        cols = lax.broadcasted_iota(jnp.int32, (seg_rows, slots_wide), 1)
        col_slot = (cols // rank) % NY * NZ + cols // (rank * NY)
        for p in range(NY):
            arrived(sin.at[p], sin_r.at[p])
            arrived(rtn.at[p], rtn_r.at[p])
            for k, lanes in enumerate(segments):
                spread_out = tn_dot(rtn[p, :, lanes], spread)
                ids = jnp.broadcast_to(sin[p, k:k + 1, 0:1], spread_out.shape)
                rx[pl.ds(p * rows + k * seg_rows, seg_rows), :] = jnp.where(
                    ids == col_slot, spread_out, 0.0
                ).astype(BF16)

    def g_wait():
        for q in x_peers:
            for p in range(NY):
                arrived(g_block(q, p), g_r.at[q, p])

    def product(i):
        place = block(y * NZ + i, chunk)

        @pl.loop(0, NY)
        def _(p):
            r = block(p, rows)
            total = nn_dot(rx[r, :], dn[:, :, block(i, chunk)].reshape(slots_wide, chunk))
            for q in range(NX):
                total += nt_dot(gf[q, r, :], wn[i, :, q * rows:(q + 1) * rows])
            ot[i, r, :] = total.astype(BF16)

        for k, p in enumerate(y_peers):
            copy(ot.at[i, block(p, rows)], out.at[:, place], o_s.at[k, i], o_r.at[y, i], at(y_=p)).start()
        out[:, place] = ot[i, block(y, rows), :]

    def product_step(t):
        for side, i in enumerate((z - t, z + t) if t else (z,)):
            @pl.when(i >= 0 if side == 0 else i < NZ)
            def _():
                if t == NZ - 1:
                    for p in range(NP):
                        arrived(w_piece(i, p), w_r.at[i, p])
                product(i)

    def product0():
        product_step(0)

    def product1():
        product_step(1)

    def product2():
        product_step(2)

    def product3():
        product_step(3)
        for i in range(NZ):
            for k in range(3):
                started.append((who[0], None, lambda: ot.at[0, block(0, rows)], (o_s, k, i)))

    def out_end():
        for p in y_peers:
            for i in range(NZ):
                arrived(out.at[:, block(p * NZ + i, chunk)], o_r.at[p, i])

    def w_step1():
        w_step(1)

    def w_step2():
        w_step(2)

    on(1, slots_out, up_out, g_shift)
    on(0, slots_out)
    on(1, slots_next_out)
    on(0, g_shift)
    on(1, w_shift)
    on(0, far0, up_out, far1, g_start_y)
    on(None, picks)
    on(0, w_start, slots_next_out)
    on(1, down_out)
    on(None, up_pick)
    on(0, down_out)
    on(None, rank_part, rank_sum, down_part)
    on(0, g_start_x, w_shift)
    on(1, g_start_y)
    on(0, down_wait, g_relay)
    on(1, down_wait)
    on(None, down_pick)
    on(0, w_step1)
    on(1, g_start_x)
    on(0, far2)
    on(1, g_relay, dn_start, w_start, down_next)
    on(None, down_sum)
    on(1, rank_spread)
    on(0, w_step2, rank_spread, g_wait, dn_wait0)
    on(1, w_step1)
    on(0, product0, product1)
    on(None, hidden_part)
    on(1, dn_relay)
    on(0, product2)
    on(1, w_step2, g_wait, dn_wait1)
    on(None, down_hop1, up_part)
    on(1, product0, product1)
    on(0, product3)
    on(None, down_hop2)
    on(1, product2, product3)
    on(None, up_sum, up_end, down_end, out_end)

    for core in (None, 0, 1):
        group = [e[1:] for e in started if e[0] == core]

        def finish():
            for when, like, ss in group:
                def wait():
                    sent(like() if callable(like) else like, ss[0].at[ss[1:]])

                if when is None:
                    wait()
                else:
                    pl.when(when())(wait)

        on(core, finish)


def body(
    activations,
    value_gradient,
    value_matrix,
    adapter_down_weight,
    adapter_up_weight,
    segment_adapter,
    adapter_slot,
):
    rows, width = activations.shape[1:]
    values = value_gradient.shape[2]
    w_rows, v_width = value_matrix.shape[1:]
    rank = adapter_down_weight.shape[2]
    slots = adapter_slot.shape[0]
    piece = width // NY
    vmem = pl.BlockSpec(memory_space=pltpu.VMEM)
    hbm = pl.BlockSpec(memory_space=pltpu.HBM)
    smem = pl.BlockSpec(memory_space=pltpu.SMEM)
    dma = lambda *shape: pltpu.SemaphoreType.DMA(shape)
    scratch = [
        pltpu.VMEM((rows, width), BF16),
        pltpu.VMEM((rows, values), BF16),
        pltpu.VMEM((NZ, w_rows, v_width), BF16),
        pltpu.VMEM((NX, NY * rows, values), BF16),
        pltpu.VMEM((rank, width), BF16),
        pltpu.VMEM((2, rank, width), BF16),
        pltpu.VMEM((NZ, NY * rank, piece), BF16),
        pltpu.VMEM((NY, 8, 128), jnp.int32),
        pltpu.VMEM((NY, 8, 128), jnp.int32),
        pltpu.VMEM((NZ, rank, values), BF16),
        pltpu.VMEM((NY * 2 * rank, values), BF16),
        pltpu.VMEM((NY, 2 * rank, values), BF16),
        pltpu.VMEM((NZ, rank, width), BF16),
        pltpu.VMEM((NY * 2 * rank, width), BF16),
        pltpu.VMEM((NY, 2 * rank, width), BF16),
        pltpu.VMEM((NY * 2 * rank, NZ * rank), BF16),
        pltpu.VMEM((NX, rank, rows), F32),
        pltpu.VMEM((rank, rows), BF16),
        pltpu.VMEM((NY, rank, rows), BF16),
        pltpu.VMEM((NY * rows, slots * rank), BF16),
        pltpu.VMEM((NX, rank, rows), F32),
        pltpu.VMEM((rank, rows), BF16),
        pltpu.VMEM((NY, 2 * rank, width), BF16),
        pltpu.VMEM((NZ, rank, width), BF16),
        pltpu.VMEM((2, NZ, rank, width), BF16),
        pltpu.VMEM((NY, 2 * rank, values), BF16),
        pltpu.VMEM((NZ * rank, values), BF16),
        pltpu.VMEM((NZ, rank, values), BF16),
        pltpu.VMEM((NZ, NY * rows, w_rows), BF16),
        dma(4), dma(NP + 1), dma(NZ, NP), dma(2, NZ, NP),
        dma(NX, NY), dma(3), dma(3, NY), dma(2), dma(3),
        pltpu.SemaphoreType.DMA, dma(NY), dma(NY + 3), dma(NZ), dma(3),
        dma(NY), dma(3), dma(NY), dma(NY),
        dma(NZ), dma(3), dma(NY), dma(3),
        dma(NZ), dma(3), dma(NY), dma(3),
        dma(NX), dma(3), dma(NY), dma(NY),
        dma(NX), dma(3), dma(NY), dma(3), dma(2, NZ), dma(2, NZ),
        dma(NY), dma(3), dma(NZ), dma(3),
        dma(NY, NZ), dma(3, NZ),
    ]
    inputs = [
        pltpu.with_memory_space_constraint(a, pltpu.HBM)
        for a in (
            activations[0], value_gradient[0], value_matrix[0], adapter_down_weight[0, 0], adapter_up_weight[0, 0]
        )
    ]
    received, down_gradient, up_gradient = pl.pallas_call(
        kernel,
        out_shape=(
            jax.ShapeDtypeStruct((rows, width), BF16),
            jax.ShapeDtypeStruct((rank, width), BF16),
            jax.ShapeDtypeStruct((rank, values), BF16),
        ),
        in_specs=[hbm] * 5 + [smem] * 2,
        out_specs=(vmem, vmem, vmem),
        scratch_shapes=scratch,
        compiler_params=pltpu.CompilerParams(
            collective_id=0, has_side_effects=True, vmem_limit_bytes=40 << 20
        ),
        name="relay_backward",
    )(
        *inputs,
        segment_adapter[0],
        adapter_slot,
    )
    return received[None], down_gradient[None, None], up_gradient[None, None]


def solution(mesh):
    placed = (
        P("section", "dp", "mp"),
        P("section", "dp", "mp"),
        P("section", ("mp", "dp"), None),
        P("section", "dp", None, "mp"),
        P("section", "dp", None, "mp"),
        P("section", "dp"),
        P(),
    )
    return jax.shard_map(
        body,
        mesh=mesh,
        in_specs=placed,
        out_specs=(
            P("section", "dp", "mp"),
            P("section", "dp", None, "mp"),
            P("section", "dp", None, "mp"),
        ),
        check_vma=False,
    )
```

```python
import functools
import math

import jax
import jax.numpy as jnp
from jax import lax
from jax.experimental import pallas as pl
from jax.experimental.pallas import tpu as pltpu
from jax.sharding import PartitionSpec as P

ADAPTERS_PER_DP = 1
ADAPTER_SCALE = 2.0
MESH = pl.DeviceIdType.MESH
BF16 = jnp.bfloat16
F32 = jnp.float32

NY = 4
NZ = 4
NX = 4
NS = 8
NP = 2


def nt_dot(a, b):
    return lax.dot_general(a, b, (((1,), (1,)), ((), ())), preferred_element_type=F32)


def nn_dot(a, b):
    return lax.dot_general(a, b, (((1,), (0,)), ((), ())), preferred_element_type=F32)


def tn_dot(a, b):
    return lax.dot_general(a, b, (((0,), (0,)), ((), ())), preferred_element_type=F32)


def kernel(
    act_hbm, grad_hbm, wmat, down, up, seg, slot,
    out, dgrad, ugrad,
    act, grad, wn, gf, dns, far, dn, si, sin, uz, usel, ur, dz, dsel, dr,
    pm, rp, rt, rtn, rx, hp, ht, pd, st, rsd, pu, su, rsu, ot,
    local_s, shift_s, w_r, w_s, g_r, g_sy, g_sx, far_r, far_s, dns_r, dna_r, dna_s, dnz_r, dnz_s,
    si_r, si_s, sin_r, sin_s, uz_r, uz_s, ur_r, ur_s, dz_r, dz_s, dr_r, dr_s,
    rp_r, rp_s, rtn_r, rtn_s, hp_r, hp_s, pd_r, pd_s, rsd_r, rsd_s,
    pu_r, pu_s, rsu_r, rsu_s, o_r, o_s,
):
    s = lax.axis_index("section")
    d = lax.axis_index("dp")
    x = lax.axis_index("mp")
    y, z = d // NZ, d % NZ
    before, after = (s + NS - 1) % NS, (s + 1) % NS
    rows = act.shape[0]
    seg_rows = rows // 2
    rank = down.shape[0]
    piece = dn.shape[2]
    chunk = wmat.shape[0]
    wp = chunk // NP
    norm = ADAPTER_SCALE / math.sqrt(rows / ADAPTERS_PER_DP)

    def at(s_=s, y_=y, z_=z, x_=x):
        return {"section": s_, "dp": y_ * NZ + z_, "mp": x_}

    def copy(src, dst, ss, rs, device):
        return pltpu.make_async_remote_copy(
            src_ref=src, dst_ref=dst, send_sem=ss, recv_sem=rs,
            device_id=device, device_id_type=MESH,
        )

    def arrived(dst, rs):
        copy(dst, dst, rs, rs, at()).wait_recv()

    def sent(src, ss):
        copy(src, src, ss, ss, at()).wait_send()

    def block(i, n):
        return pl.ds(i * n, n) if isinstance(i, int) else pl.ds(pl.multiple_of(i * n, n), n)

    y_peers = [(y + k) % NY for k in (1, 3, 2)]
    x_peers = [(x + k) % NX for k in (1, 3, 2)]
    z_peers = [(z + k) % NZ for k in (1, 2, 3)]
    segments = [slice(k * seg_rows, (k + 1) * seg_rows) for k in range(2)]
    ranks = [slice(k * rank, (k + 1) * rank) for k in range(2)]
    wide = 2 * rank
    columns = [slice(j, j + 512) for j in range(0, act.shape[1], 512)]
    who = [None]
    started = []

    def send(like, src, dst, ss, rs, device, when=None):
        started.append((who[0], when, like, ss))

        def start():
            copy(src, dst, ss[0].at[ss[1:]], rs, device).start()

        if when is None:
            start()
        else:
            pl.when(when())(start)

    def on(core, *steps):
        who[0] = core

        def run():
            for step in steps:
                step()

        if core is None:
            run()
        else:
            pl.when(s % 2 == core)(run)
        who[0] = None

    loads = [
        pltpu.make_async_copy(src, dst, local_s.at[k])
        for k, (src, dst) in enumerate(
            [(up, uz.at[z]), (grad_hbm, grad), (down, dz.at[z]), (act_hbm, act)]
        )
    ]
    for load in loads:
        load.start()

    bar = pltpu.get_barrier_semaphore()
    senders = (
        [at(y_=p) for p in y_peers] + [at(x_=p) for p in x_peers] + [at(z_=p) for p in z_peers]
        + [at(s_=after, y_=k) for k in range(NY)] + [at(s_=(s + 6 - s % 2) % NS)]
    )
    for p in senders:
        pl.semaphore_signal(bar, inc=1, device_id=p, device_id_type=MESH)
    si[y, 0:1, :] = jnp.full((1, 128), slot[seg[0]], jnp.int32)
    si[y, 1:2, :] = jnp.full((1, 128), slot[seg[1]], jnp.int32)
    pl.semaphore_wait(bar, 9 + NY + 2 * (1 - s % 2))

    def g_block(x_, y_):
        return gf.at[x_, block(y_, rows)]

    def w_piece(i, p):
        return wn.at[i, p * wp:(p + 1) * wp]

    def slots_out():
        for k, p in enumerate(y_peers):
            send(lambda: si.at[0], si.at[y], si.at[y], (si_s, k), si_r.at[y], at(y_=p))

    def up_out():
        for k, p in enumerate(z_peers):
            send(up, up, uz.at[z], (uz_s, k), uz_r.at[z], at(z_=p))

    def down_out():
        for k, p in enumerate(z_peers):
            send(down, down, dz.at[z], (dz_s, k), dz_r.at[z], at(z_=p))

    def slots_next_out():
        for k in range(NY):
            send(lambda: si.at[0], si.at[y], sin.at[y], (sin_s, k), sin_r.at[y], at(s_=before, y_=k))

    def w_shift():
        for p in range(NP):
            send(lambda p=p: w_piece(0, p), wmat.at[p * wp:(p + 1) * wp], w_piece(z, p), (shift_s, p), w_r.at[z, p], at(s_=before))

    def g_shift():
        send(grad, grad_hbm, g_block(x, y), (shift_s, NP), g_r.at[x, y], at(s_=before))

    def far0():
        send(down, down, far.at[0], (far_s, 0), far_r.at[0], at(s_=(s + 2) % NS))

    def far1():
        arrived(far.at[0], far_r.at[0])
        send(dns, far.at[0], far.at[1], (far_s, 1), far_r.at[1], at(s_=(s + 2) % NS))

    def far2():
        arrived(far.at[1], far_r.at[1])
        send(dns, far.at[1], dns, (far_s, 2), dns_r, at(s_=(s + 3) % NS))

    def g_start_y():
        arrived(g_block(x, y), g_r.at[x, y])
        for k, p in enumerate(y_peers):
            send(grad, g_block(x, y), g_block(x, y), (g_sy, k), g_r.at[x, y], at(y_=p))

    def g_start_x():
        for k, p in enumerate(x_peers):
            send(grad, g_block(x, y), g_block(x, y), (g_sx, k, 0), g_r.at[x, y], at(x_=p))

    def g_relay():
        for j, p in enumerate(y_peers):
            arrived(g_block(x, p), g_r.at[x, p])
            for k, q in enumerate(x_peers):
                send(grad, g_block(x, p), g_block(x, p), (g_sx, k, 1 + j), g_r.at[x, p], at(x_=q))

    def w_out(t, p, way):
        i, z_to = (z - t, z + 1) if way == 0 else (z + t, z - 1)

        def when():
            if way == 0:
                return jnp.logical_and(z < NZ - 1, z >= t)
            return jnp.logical_and(z > 0, z < NZ - t)

        send(lambda p=p: w_piece(0, p), w_piece(i, p), w_piece(i, p), (w_s, way, t, p), w_r.at[i, p], at(z_=z_to), when)

    def w_start():
        for p in range(NP):
            arrived(w_piece(z, p), w_r.at[z, p])
            w_out(0, p, 1)
            w_out(0, p, 0)

    def w_step(t):
        lo, hi = z - t, z + t
        for p in range(NP):
            pl.when(hi < NZ)(functools.partial(arrived, w_piece(hi, p), w_r.at[hi, p]))
            w_out(t, p, 1)
            pl.when(lo >= 0)(functools.partial(arrived, w_piece(lo, p), w_r.at[lo, p]))
            w_out(t, p, 0)

    def picks():
        for p in y_peers:
            arrived(si.at[p], si_r.at[p])
        col = lax.broadcasted_iota(jnp.int32, (rank, 128), 1)
        row = lax.broadcasted_iota(jnp.int32, (rank, 128), 0)
        same = row == col % rank
        here = y * NZ + col // rank
        for p in range(NY):
            for k in range(2):
                ids = jnp.broadcast_to(si[p, k:k + 1, :], (rank, 128))
                hit = jnp.where(jnp.logical_and(ids == here, same), 1.0, 0.0)
                pm[pl.ds((p * 2 + k) * rank, rank), :] = hit.astype(BF16)

    def up_pick():
        loads[0].wait()
        for p in z_peers:
            arrived(uz.at[p], uz_r.at[p])
        usel[...] = nn_dot(pm[...], uz[...].reshape(NZ * rank, up.shape[1])).astype(BF16)
        for k, p in enumerate(y_peers):
            send(lambda: ur.at[0], usel.at[block(p, wide)], ur.at[y], (ur_s, k), ur_r.at[y], at(y_=p))
        ur[y] = usel[block(y, wide), :]

    def rank_part():
        loads[1].wait()
        for p in y_peers:
            arrived(ur.at[p], ur_r.at[p])
        picked = sum(ur[p].astype(F32) for p in range(NY)).astype(BF16)
        for r, lanes in zip(ranks, segments):
            rp[x, :, lanes] = nt_dot(picked[r], grad[lanes, :])
        for k, p in enumerate(x_peers):
            send(lambda: rp.at[0], rp.at[x], rp.at[x], (rp_s, k), rp_r.at[x], at(x_=p))

    def rank_sum():
        for p in x_peers:
            arrived(rp.at[p], rp_r.at[p])
        rt[...] = sum(rp[p] for p in range(NX)).astype(BF16)
        for k in range(NY):
            send(rt, rt, rtn.at[y], (rtn_s, k), rtn_r.at[y], at(s_=before, y_=k))

    def down_part():
        loads[3].wait()
        for r, lanes in zip(ranks, segments):
            pd[y, r, :] = (nn_dot(rt[:, lanes], act[lanes, :]) * norm).astype(BF16)
        for k, p in enumerate(y_peers):
            send(lambda: pd.at[0], pd.at[y], pd.at[y], (pd_s, k), pd_r.at[y], at(y_=p))

    def down_way(way, q, when):
        z_to = z - 1 if way == 0 else z + 1
        send(lambda: rsd.at[0, 0], rsd.at[way, q], rsd.at[way, q], (rsd_s, way, q), rsd_r.at[way, q], at(z_=z_to), when)

    def down_sum():
        for p in y_peers:
            arrived(pd.at[p], pd_r.at[p])
        for c in columns:
            st[:, :, c] = tn_dot(pm[...], pd[:, :, c].reshape(NY * wide, 512)).astype(BF16).reshape(NZ, rank, 512)

        @pl.when(z == NZ - 1)
        def _():
            for q in range(NZ - 1):
                rsd[0, q] = st[q]

        @pl.when(z == 0)
        def _():
            for q in range(1, NZ):
                rsd[1, q] = st[q]

        for q in range(NZ - 1):
            down_way(0, q, lambda: z == NZ - 1)
        for q in range(NZ - 1, 0, -1):
            down_way(1, q, lambda: z == 0)

    def down_hop(way, q, here):
        @pl.when(z == here)
        def _():
            arrived(rsd.at[way, q], rsd_r.at[way, q])
            rsd[way, q] = (rsd[way, q].astype(F32) + st[q].astype(F32)).astype(BF16)

        down_way(way, q, lambda: z == here)

    def down_hop1():
        for k in range(2):
            down_hop(0, k, 2)
            down_hop(1, 3 - k, 1)

    def down_hop2():
        down_hop(0, 0, 1)
        down_hop(1, 3, 2)

    def down_end():
        pl.when(z < NZ - 1)(lambda: arrived(rsd.at[0, z], rsd_r.at[0, z]))
        pl.when(z > 0)(lambda: arrived(rsd.at[1, z], rsd_r.at[1, z]))
        total = st[z].astype(F32)
        total += jnp.where(z < NZ - 1, rsd[0, z].astype(F32), 0.0)
        total += jnp.where(z > 0, rsd[1, z].astype(F32), 0.0)
        dgrad[...] = total.astype(BF16)

    def down_wait():
        loads[2].wait()
        for p in z_peers:
            arrived(dz.at[p], dz_r.at[p])

    def down_next():
        for k in range(NY):
            send(lambda: dn.at[:, block(0, rank)], dz.at[:, :, block(k, piece)], dn.at[:, block(y, rank)],
                 (dna_s, k), dna_r.at[y], at(s_=before, y_=k))

    def down_pick():
        for c in columns:
            dsel[:, c] = nn_dot(pm[...], dz[:, :, c].reshape(NZ * rank, 512)).astype(BF16)
        for k, p in enumerate(y_peers):
            send(lambda: dr.at[0], dsel.at[block(p, wide)], dr.at[y], (dr_s, k), dr_r.at[y], at(y_=p))
        dr[y] = dsel[block(y, wide), :]

    def hidden_part():
        for p in y_peers:
            arrived(dr.at[p], dr_r.at[p])
        for r, lanes in zip(ranks, segments):
            picked = sum(dr[p, r, :].astype(F32) for p in range(NY)).astype(BF16)
            hp[x, :, lanes] = nt_dot(picked, act[lanes, :])
        for k, p in enumerate(x_peers):
            send(lambda: hp.at[0], hp.at[x], hp.at[x], (hp_s, k), hp_r.at[x], at(x_=p))

    def up_part():
        for p in x_peers:
            arrived(hp.at[p], hp_r.at[p])
        ht[...] = sum(hp[p] for p in range(NX)).astype(BF16)
        for r, lanes in zip(ranks, segments):
            pu[y, r, :] = (nn_dot(ht[:, lanes], grad[lanes, :]) * norm).astype(BF16)
        for k, p in enumerate(y_peers):
            send(lambda: pu.at[0], pu.at[y], pu.at[y], (pu_s, k), pu_r.at[y], at(y_=p))

    def up_sum():
        for p in y_peers:
            arrived(pu.at[p], pu_r.at[p])
        su[...] = tn_dot(pm[...], pu[...].reshape(NY * wide, up.shape[1])).astype(BF16)
        for k, p in enumerate(z_peers):
            send(lambda: rsu.at[0], su.at[block(p, rank)], rsu.at[z], (rsu_s, k), rsu_r.at[z], at(z_=p))
        rsu[z] = su[block(z, rank), :]

    def up_end():
        for p in z_peers:
            arrived(rsu.at[p], rsu_r.at[p])
        ugrad[...] = sum(rsu[p].astype(F32) for p in range(NZ)).astype(BF16)

    def dn_start():
        arrived(dns, dns_r)
        for k, p in enumerate(y_peers):
            send(lambda: dn.at[0, block(0, rank)], dns.at[:, block(p, piece)], dn.at[z, block(y, rank)],
                 (dna_s, NY + k), dna_r.at[y], at(y_=p))
        dn[z, block(y, rank), :] = dns[:, block(y, piece)]

    def dn_relay():
        for p in y_peers:
            arrived(dn.at[z, block(p, rank)], dna_r.at[p])
        for k, p in enumerate(z_peers):
            send(lambda: dn.at[0], dn.at[z], dn.at[z], (dnz_s, k), dnz_r.at[z], at(z_=p))

    def dn_wait0():
        for p in range(NY):
            arrived(dn.at[:, block(p, rank)], dna_r.at[p])

    def dn_wait1():
        for p in z_peers:
            arrived(dn.at[p], dnz_r.at[p])

    slots_wide = rx.shape[1]

    def rank_spread():
        spread = jnp.where(
            lax.broadcasted_iota(jnp.int32, (rank, slots_wide), 0)
            == lax.broadcasted_iota(jnp.int32, (rank, slots_wide), 1) % rank,
            ADAPTER_SCALE, 0.0,
        ).astype(BF16)
        cols = lax.broadcasted_iota(jnp.int32, (seg_rows, slots_wide), 1)
        col_slot = (cols // rank) % NY * NZ + cols // (rank * NY)
        for p in range(NY):
            arrived(sin.at[p], sin_r.at[p])
            arrived(rtn.at[p], rtn_r.at[p])
            for k, lanes in enumerate(segments):
                spread_out = tn_dot(rtn[p, :, lanes], spread)
                ids = jnp.broadcast_to(sin[p, k:k + 1, 0:1], spread_out.shape)
                rx[pl.ds(p * rows + k * seg_rows, seg_rows), :] = jnp.where(
                    ids == col_slot, spread_out, 0.0
                ).astype(BF16)

    def g_wait():
        for q in x_peers:
            for p in range(NY):
                arrived(g_block(q, p), g_r.at[q, p])

    def product(i):
        place = block(y * NZ + i, chunk)

        total = nn_dot(rx[...], dn[:, :, block(i, chunk)].reshape(slots_wide, chunk))
        for q in range(NX):
            total += nt_dot(gf[q], wn[i, :, q * rows:(q + 1) * rows])
        ot[i] = total.astype(BF16)

        for k, p in enumerate(y_peers):
            copy(ot.at[i, block(p, rows)], out.at[:, place], o_s.at[k, i], o_r.at[y, i], at(y_=p)).start()
        out[:, place] = ot[i, block(y, rows), :]

    def product_step(t):
        for side, i in enumerate((z - t, z + t) if t else (z,)):
            @pl.when(i >= 0 if side == 0 else i < NZ)
            def _():
                if t == NZ - 1:
                    for p in range(NP):
                        arrived(w_piece(i, p), w_r.at[i, p])
                product(i)

    def product0():
        product_step(0)

    def product1():
        product_step(1)

    def product2():
        product_step(2)

    def product3():
        product_step(3)
        for i in range(NZ):
            for k in range(3):
                started.append((who[0], None, lambda: ot.at[0, block(0, rows)], (o_s, k, i)))

    def out_end():
        for p in y_peers:
            for i in range(NZ):
                arrived(out.at[:, block(p * NZ + i, chunk)], o_r.at[p, i])

    def w_step1():
        w_step(1)

    def w_step2():
        w_step(2)

    on(None, slots_out, up_out, w_shift, g_shift)
    on(0, far0, w_start)
    on(None, down_out)
    on(None, picks, up_pick)
    on(0, g_start_y, far1)
    on(None, rank_part)
    on(0, g_start_x)
    on(None, rank_sum, down_part, slots_next_out)
    on(0, g_relay)
    on(1, w_start)
    on(0, w_step1, far2)
    on(1, g_start_y, g_start_x)
    on(None, down_wait)
    on(None, down_pick)
    on(1, down_next)
    on(1, w_step1)
    on(0, w_step2, rank_spread)
    on(1, g_relay)
    on(None, down_sum)
    on(1, dn_start, w_step2, rank_spread)
    on(None, down_hop1, hidden_part)
    on(1, dn_relay)
    on(0, dn_wait0, g_wait, product0, product1, product2)
    on(None, down_hop2, up_part)
    on(1, dn_wait1, g_wait)
    on(0, product3)
    on(1, product0, product1, product2, product3)
    on(None, up_sum, down_end, up_end, out_end)

    for core in (None, 0, 1):
        group = [e[1:] for e in started if e[0] == core]

        def finish():
            for when, like, ss in group:
                def wait():
                    sent(like() if callable(like) else like, ss[0].at[ss[1:]])

                if when is None:
                    wait()
                else:
                    pl.when(when())(wait)

        on(core, finish)


def body(
    activations,
    value_gradient,
    value_matrix,
    adapter_down_weight,
    adapter_up_weight,
    segment_adapter,
    adapter_slot,
):
    rows, width = activations.shape[1:]
    values = value_gradient.shape[2]
    w_rows, v_width = value_matrix.shape[1:]
    rank = adapter_down_weight.shape[2]
    slots = adapter_slot.shape[0]
    piece = width // NY
    vmem = pl.BlockSpec(memory_space=pltpu.VMEM)
    hbm = pl.BlockSpec(memory_space=pltpu.HBM)
    smem = pl.BlockSpec(memory_space=pltpu.SMEM)
    dma = lambda *shape: pltpu.SemaphoreType.DMA(shape)
    scratch = [
        pltpu.VMEM((rows, width), BF16),
        pltpu.VMEM((rows, values), BF16),
        pltpu.VMEM((NZ, w_rows, v_width), BF16),
        pltpu.VMEM((NX, NY * rows, values), BF16),
        pltpu.VMEM((rank, width), BF16),
        pltpu.VMEM((2, rank, width), BF16),
        pltpu.VMEM((NZ, NY * rank, piece), BF16),
        pltpu.VMEM((NY, 8, 128), jnp.int32),
        pltpu.VMEM((NY, 8, 128), jnp.int32),
        pltpu.VMEM((NZ, rank, values), BF16),
        pltpu.VMEM((NY * 2 * rank, values), BF16),
        pltpu.VMEM((NY, 2 * rank, values), BF16),
        pltpu.VMEM((NZ, rank, width), BF16),
        pltpu.VMEM((NY * 2 * rank, width), BF16),
        pltpu.VMEM((NY, 2 * rank, width), BF16),
        pltpu.VMEM((NY * 2 * rank, NZ * rank), BF16),
        pltpu.VMEM((NX, rank, rows), F32),
        pltpu.VMEM((rank, rows), BF16),
        pltpu.VMEM((NY, rank, rows), BF16),
        pltpu.VMEM((NY * rows, slots * rank), BF16),
        pltpu.VMEM((NX, rank, rows), F32),
        pltpu.VMEM((rank, rows), BF16),
        pltpu.VMEM((NY, 2 * rank, width), BF16),
        pltpu.VMEM((NZ, rank, width), BF16),
        pltpu.VMEM((2, NZ, rank, width), BF16),
        pltpu.VMEM((NY, 2 * rank, values), BF16),
        pltpu.VMEM((NZ * rank, values), BF16),
        pltpu.VMEM((NZ, rank, values), BF16),
        pltpu.VMEM((NZ, NY * rows, w_rows), BF16),
        dma(4), dma(NP + 1), dma(NZ, NP), dma(2, NZ, NP),
        dma(NX, NY), dma(3), dma(3, NY), dma(2), dma(3),
        pltpu.SemaphoreType.DMA, dma(NY), dma(NY + 3), dma(NZ), dma(3),
        dma(NY), dma(3), dma(NY), dma(NY),
        dma(NZ), dma(3), dma(NY), dma(3),
        dma(NZ), dma(3), dma(NY), dma(3),
        dma(NX), dma(3), dma(NY), dma(NY),
        dma(NX), dma(3), dma(NY), dma(3), dma(2, NZ), dma(2, NZ),
        dma(NY), dma(3), dma(NZ), dma(3),
        dma(NY, NZ), dma(3, NZ),
    ]
    inputs = [
        pltpu.with_memory_space_constraint(a, pltpu.HBM)
        for a in (
            activations[0], value_gradient[0], value_matrix[0], adapter_down_weight[0, 0], adapter_up_weight[0, 0]
        )
    ]
    received, down_gradient, up_gradient = pl.pallas_call(
        kernel,
        out_shape=(
            jax.ShapeDtypeStruct((rows, width), BF16),
            jax.ShapeDtypeStruct((rank, width), BF16),
            jax.ShapeDtypeStruct((rank, values), BF16),
        ),
        in_specs=[hbm] * 5 + [smem] * 2,
        out_specs=(vmem, vmem, vmem),
        scratch_shapes=scratch,
        compiler_params=pltpu.CompilerParams(
            collective_id=0, has_side_effects=True, vmem_limit_bytes=40 << 20
        ),
        name="relay_backward",
    )(
        *inputs,
        segment_adapter[0],
        adapter_slot,
    )
    return received[None], down_gradient[None, None], up_gradient[None, None]


def solution(mesh):
    placed = (
        P("section", "dp", "mp"),
        P("section", "dp", "mp"),
        P("section", ("mp", "dp"), None),
        P("section", "dp", None, "mp"),
        P("section", "dp", None, "mp"),
        P("section", "dp"),
        P(),
    )
    return jax.shard_map(
        body,
        mesh=mesh,
        in_specs=placed,
        out_specs=(
            P("section", "dp", "mp"),
            P("section", "dp", None, "mp"),
            P("section", "dp", None, "mp"),
        ),
        check_vma=False,
    )
```

```python
import functools
import math

import jax
import jax.numpy as jnp
from jax import lax
from jax.experimental import pallas as pl
from jax.experimental.pallas import tpu as pltpu
from jax.sharding import PartitionSpec as P

ADAPTERS_PER_DP = 1
ADAPTER_SCALE = 2.0
MESH = pl.DeviceIdType.MESH
BF16 = jnp.bfloat16
F32 = jnp.float32

NY = 4
NZ = 4
NX = 4
NS = 8
NP = 2


def nt_dot(a, b):
    return lax.dot_general(a, b, (((1,), (1,)), ((), ())), preferred_element_type=F32)


def nn_dot(a, b):
    return lax.dot_general(a, b, (((1,), (0,)), ((), ())), preferred_element_type=F32)


def tn_dot(a, b):
    return lax.dot_general(a, b, (((0,), (0,)), ((), ())), preferred_element_type=F32)


def kernel(
    act_hbm, grad_hbm, wmat, down, up, seg, slot,
    out, dgrad, ugrad,
    act, grad, wn, gf, dns, far, dn, si, sin, uz, usel, ur, dz, dsel, dr,
    pm, rp, rt, rtn, rx, hp, ht, pd, st, rsd, pu, su, rsu, ot,
    local_s, shift_s, w_r, w_s, g_r, g_sy, g_sx, far_r, far_s, dns_r, dna_r, dna_s, dnz_r, dnz_s,
    si_r, si_s, sin_r, sin_s, uz_r, uz_s, ur_r, ur_s, dz_r, dz_s, dr_r, dr_s,
    rp_r, rp_s, rtn_r, rtn_s, hp_r, hp_s, pd_r, pd_s, rsd_r, rsd_s,
    pu_r, pu_s, rsu_r, rsu_s, o_r, o_s,
):
    s = lax.axis_index("section")
    d = lax.axis_index("dp")
    x = lax.axis_index("mp")
    y, z = d // NZ, d % NZ
    before, after = (s + NS - 1) % NS, (s + 1) % NS
    rows = act.shape[0]
    seg_rows = rows // 2
    rank = down.shape[0]
    piece = dn.shape[2]
    chunk = wmat.shape[0]
    wp = chunk // NP
    norm = ADAPTER_SCALE / math.sqrt(rows / ADAPTERS_PER_DP)

    def at(s_=s, y_=y, z_=z, x_=x):
        return {"section": s_, "dp": y_ * NZ + z_, "mp": x_}

    def copy(src, dst, ss, rs, device):
        return pltpu.make_async_remote_copy(
            src_ref=src, dst_ref=dst, send_sem=ss, recv_sem=rs,
            device_id=device, device_id_type=MESH,
        )

    def arrived(dst, rs):
        copy(dst, dst, rs, rs, at()).wait_recv()

    def sent(src, ss):
        copy(src, src, ss, ss, at()).wait_send()

    def block(i, n):
        return pl.ds(i * n, n) if isinstance(i, int) else pl.ds(pl.multiple_of(i * n, n), n)

    y_peers = [(y + k) % NY for k in (1, 3, 2)]
    x_peers = [(x + k) % NX for k in (1, 3, 2)]
    z_peers = [(z + k) % NZ for k in (1, 2, 3)]
    segments = [slice(k * seg_rows, (k + 1) * seg_rows) for k in range(2)]
    ranks = [slice(k * rank, (k + 1) * rank) for k in range(2)]
    wide = 2 * rank
    columns = [slice(j, j + 512) for j in range(0, act.shape[1], 512)]
    who = [None]
    started = []

    def send(like, src, dst, ss, rs, device, when=None):
        started.append((who[0], when, like, ss))

        def start():
            copy(src, dst, ss[0].at[ss[1:]], rs, device).start()

        if when is None:
            start()
        else:
            pl.when(when())(start)

    def on(core, *steps):
        who[0] = core

        def run():
            for step in steps:
                step()

        if core is None:
            run()
        else:
            pl.when(s % 2 == core)(run)
        who[0] = None

    loads = [
        pltpu.make_async_copy(src, dst, local_s.at[k])
        for k, (src, dst) in enumerate(
            [(up, uz.at[z]), (grad_hbm, grad), (down, dz.at[z]), (act_hbm, act)]
        )
    ]
    for load in loads:
        load.start()

    bar = pltpu.get_barrier_semaphore()
    senders = (
        [at(y_=p) for p in y_peers] + [at(x_=p) for p in x_peers] + [at(z_=p) for p in z_peers]
        + [at(s_=after, y_=k) for k in range(NY)] + [at(s_=(s + 6 - s % 2) % NS)]
    )
    for p in senders:
        pl.semaphore_signal(bar, inc=1, device_id=p, device_id_type=MESH)
    si[y, 0:1, :] = jnp.full((1, 128), slot[seg[0]], jnp.int32)
    si[y, 1:2, :] = jnp.full((1, 128), slot[seg[1]], jnp.int32)
    pl.semaphore_wait(bar, 9 + NY + 2 * (1 - s % 2))

    def g_block(x_, y_):
        return gf.at[x_, block(y_, rows)]

    def w_piece(i, p):
        return wn.at[i, p * wp:(p + 1) * wp]

    def slots_out():
        for k, p in enumerate(y_peers):
            send(lambda: si.at[0], si.at[y], si.at[y], (si_s, k), si_r.at[y], at(y_=p))

    def up_out():
        for k, p in enumerate(z_peers):
            send(up, up, uz.at[z], (uz_s, k), uz_r.at[z], at(z_=p))

    def down_out():
        for k, p in enumerate(z_peers):
            send(down, down, dz.at[z], (dz_s, k), dz_r.at[z], at(z_=p))

    def slots_next_out():
        for k in range(NY):
            send(lambda: si.at[0], si.at[y], sin.at[y], (sin_s, k), sin_r.at[y], at(s_=before, y_=k))

    def w_shift():
        for p in range(NP):
            send(lambda p=p: w_piece(0, p), wmat.at[p * wp:(p + 1) * wp], w_piece(z, p), (shift_s, p), w_r.at[z, p], at(s_=before))

    def g_shift():
        send(grad, grad_hbm, g_block(x, y), (shift_s, NP), g_r.at[x, y], at(s_=before))

    def far0():
        send(down, down, far.at[0], (far_s, 0), far_r.at[0], at(s_=(s + 2) % NS))

    def far1():
        arrived(far.at[0], far_r.at[0])
        send(dns, far.at[0], far.at[1], (far_s, 1), far_r.at[1], at(s_=(s + 2) % NS))

    def far2():
        arrived(far.at[1], far_r.at[1])
        send(dns, far.at[1], dns, (far_s, 2), dns_r, at(s_=(s + 3) % NS))

    def g_start_y():
        arrived(g_block(x, y), g_r.at[x, y])
        for k, p in enumerate(y_peers):
            send(grad, g_block(x, y), g_block(x, y), (g_sy, k), g_r.at[x, y], at(y_=p))

    def g_start_x():
        for k, p in enumerate(x_peers):
            send(grad, g_block(x, y), g_block(x, y), (g_sx, k, 0), g_r.at[x, y], at(x_=p))

    def g_relay():
        for j, p in enumerate(y_peers):
            arrived(g_block(x, p), g_r.at[x, p])
            for k, q in enumerate(x_peers):
                send(grad, g_block(x, p), g_block(x, p), (g_sx, k, 1 + j), g_r.at[x, p], at(x_=q))

    def w_out(t, p, way):
        i, z_to = (z - t, z + 1) if way == 0 else (z + t, z - 1)

        def when():
            if way == 0:
                return jnp.logical_and(z < NZ - 1, z >= t)
            return jnp.logical_and(z > 0, z < NZ - t)

        send(lambda p=p: w_piece(0, p), w_piece(i, p), w_piece(i, p), (w_s, way, t, p), w_r.at[i, p], at(z_=z_to), when)

    def w_start():
        for p in range(NP):
            arrived(w_piece(z, p), w_r.at[z, p])
            w_out(0, p, 1)
            w_out(0, p, 0)

    def w_step(t):
        lo, hi = z - t, z + t
        for p in range(NP):
            pl.when(hi < NZ)(functools.partial(arrived, w_piece(hi, p), w_r.at[hi, p]))
            w_out(t, p, 1)
            pl.when(lo >= 0)(functools.partial(arrived, w_piece(lo, p), w_r.at[lo, p]))
            w_out(t, p, 0)

    def picks():
        for p in y_peers:
            arrived(si.at[p], si_r.at[p])
        col = lax.broadcasted_iota(jnp.int32, (rank, 128), 1)
        row = lax.broadcasted_iota(jnp.int32, (rank, 128), 0)
        same = row == col % rank
        here = y * NZ + col // rank
        for p in range(NY):
            for k in range(2):
                ids = jnp.broadcast_to(si[p, k:k + 1, :], (rank, 128))
                hit = jnp.where(jnp.logical_and(ids == here, same), 1.0, 0.0)
                pm[pl.ds((p * 2 + k) * rank, rank), :] = hit.astype(BF16)

    def up_pick():
        loads[0].wait()
        for p in z_peers:
            arrived(uz.at[p], uz_r.at[p])
        usel[...] = nn_dot(pm[...], uz[...].reshape(NZ * rank, up.shape[1])).astype(BF16)
        for k, p in enumerate(y_peers):
            send(lambda: ur.at[0], usel.at[block(p, wide)], ur.at[y], (ur_s, k), ur_r.at[y], at(y_=p))
        ur[y] = usel[block(y, wide), :]

    def rank_part():
        loads[1].wait()
        for p in y_peers:
            arrived(ur.at[p], ur_r.at[p])
        picked = sum(ur[p].astype(F32) for p in range(NY)).astype(BF16)
        for r, lanes in zip(ranks, segments):
            rp[x, :, lanes] = nt_dot(picked[r], grad[lanes, :])
        for k, p in enumerate(x_peers):
            send(lambda: rp.at[0], rp.at[x], rp.at[x], (rp_s, k), rp_r.at[x], at(x_=p))

    def rank_sum():
        for p in x_peers:
            arrived(rp.at[p], rp_r.at[p])
        rt[...] = sum(rp[p] for p in range(NX)).astype(BF16)
        for k in range(NY):
            send(rt, rt, rtn.at[y], (rtn_s, k), rtn_r.at[y], at(s_=before, y_=k))

    def down_part():
        loads[3].wait()
        for r, lanes in zip(ranks, segments):
            pd[y, r, :] = (nn_dot(rt[:, lanes], act[lanes, :]) * norm).astype(BF16)
        for k, p in enumerate(y_peers):
            send(lambda: pd.at[0], pd.at[y], pd.at[y], (pd_s, k), pd_r.at[y], at(y_=p))

    def down_way(way, q, when):
        z_to = z - 1 if way == 0 else z + 1
        send(lambda: rsd.at[0, 0], rsd.at[way, q], rsd.at[way, q], (rsd_s, way, q), rsd_r.at[way, q], at(z_=z_to), when)

    def down_sum():
        for p in y_peers:
            arrived(pd.at[p], pd_r.at[p])
        for c in columns:
            st[:, :, c] = tn_dot(pm[...], pd[:, :, c].reshape(NY * wide, 512)).astype(BF16).reshape(NZ, rank, 512)

        @pl.when(z == NZ - 1)
        def _():
            for q in range(NZ - 1):
                rsd[0, q] = st[q]

        @pl.when(z == 0)
        def _():
            for q in range(1, NZ):
                rsd[1, q] = st[q]

        for q in range(NZ - 1):
            down_way(0, q, lambda: z == NZ - 1)
        for q in range(NZ - 1, 0, -1):
            down_way(1, q, lambda: z == 0)

    def down_hop(way, q, here):
        @pl.when(z == here)
        def _():
            arrived(rsd.at[way, q], rsd_r.at[way, q])
            rsd[way, q] = (rsd[way, q].astype(F32) + st[q].astype(F32)).astype(BF16)

        down_way(way, q, lambda: z == here)

    def down_hop1():
        for k in range(2):
            down_hop(0, k, 2)
            down_hop(1, 3 - k, 1)

    def down_hop2():
        down_hop(0, 0, 1)
        down_hop(1, 3, 2)

    def down_end():
        pl.when(z < NZ - 1)(lambda: arrived(rsd.at[0, z], rsd_r.at[0, z]))
        pl.when(z > 0)(lambda: arrived(rsd.at[1, z], rsd_r.at[1, z]))
        total = st[z].astype(F32)
        total += jnp.where(z < NZ - 1, rsd[0, z].astype(F32), 0.0)
        total += jnp.where(z > 0, rsd[1, z].astype(F32), 0.0)
        dgrad[...] = total.astype(BF16)

    def down_wait():
        loads[2].wait()
        for p in z_peers:
            arrived(dz.at[p], dz_r.at[p])

    def down_next():
        for k in range(NY):
            send(lambda: dn.at[:, block(0, rank)], dz.at[:, :, block(k, piece)], dn.at[:, block(y, rank)],
                 (dna_s, k), dna_r.at[y], at(s_=before, y_=k))

    def down_pick():
        for c in columns:
            dsel[:, c] = nn_dot(pm[...], dz[:, :, c].reshape(NZ * rank, 512)).astype(BF16)
        for k, p in enumerate(y_peers):
            send(lambda: dr.at[0], dsel.at[block(p, wide)], dr.at[y], (dr_s, k), dr_r.at[y], at(y_=p))
        dr[y] = dsel[block(y, wide), :]

    def hidden_part():
        for p in y_peers:
            arrived(dr.at[p], dr_r.at[p])
        for r, lanes in zip(ranks, segments):
            picked = sum(dr[p, r, :].astype(F32) for p in range(NY)).astype(BF16)
            hp[x, :, lanes] = nt_dot(picked, act[lanes, :])
        for k, p in enumerate(x_peers):
            send(lambda: hp.at[0], hp.at[x], hp.at[x], (hp_s, k), hp_r.at[x], at(x_=p))

    def up_part():
        for p in x_peers:
            arrived(hp.at[p], hp_r.at[p])
        ht[...] = sum(hp[p] for p in range(NX)).astype(BF16)
        for r, lanes in zip(ranks, segments):
            pu[y, r, :] = (nn_dot(ht[:, lanes], grad[lanes, :]) * norm).astype(BF16)
        for k, p in enumerate(y_peers):
            send(lambda: pu.at[0], pu.at[y], pu.at[y], (pu_s, k), pu_r.at[y], at(y_=p))

    def up_sum():
        for p in y_peers:
            arrived(pu.at[p], pu_r.at[p])
        su[...] = tn_dot(pm[...], pu[...].reshape(NY * wide, up.shape[1])).astype(BF16)
        for k, p in enumerate(z_peers):
            send(lambda: rsu.at[0], su.at[block(p, rank)], rsu.at[z], (rsu_s, k), rsu_r.at[z], at(z_=p))
        rsu[z] = su[block(z, rank), :]

    def up_end():
        for p in z_peers:
            arrived(rsu.at[p], rsu_r.at[p])
        ugrad[...] = sum(rsu[p].astype(F32) for p in range(NZ)).astype(BF16)

    def dn_start():
        arrived(dns, dns_r)
        for k, p in enumerate(y_peers):
            send(lambda: dn.at[0, block(0, rank)], dns.at[:, block(p, piece)], dn.at[z, block(y, rank)],
                 (dna_s, NY + k), dna_r.at[y], at(y_=p))
        dn[z, block(y, rank), :] = dns[:, block(y, piece)]

    def dn_relay():
        for p in y_peers:
            arrived(dn.at[z, block(p, rank)], dna_r.at[p])
        for k, p in enumerate(z_peers):
            send(lambda: dn.at[0], dn.at[z], dn.at[z], (dnz_s, k), dnz_r.at[z], at(z_=p))

    def dn_wait0():
        for p in range(NY):
            arrived(dn.at[:, block(p, rank)], dna_r.at[p])

    def dn_wait1():
        for p in z_peers:
            arrived(dn.at[p], dnz_r.at[p])

    slots_wide = rx.shape[1]

    def rank_spread():
        spread = jnp.where(
            lax.broadcasted_iota(jnp.int32, (rank, slots_wide), 0)
            == lax.broadcasted_iota(jnp.int32, (rank, slots_wide), 1) % rank,
            ADAPTER_SCALE, 0.0,
        ).astype(BF16)
        cols = lax.broadcasted_iota(jnp.int32, (seg_rows, slots_wide), 1)
        col_slot = (cols // rank) % NY * NZ + cols // (rank * NY)
        for p in range(NY):
            arrived(sin.at[p], sin_r.at[p])
            arrived(rtn.at[p], rtn_r.at[p])
            for k, lanes in enumerate(segments):
                spread_out = tn_dot(rtn[p, :, lanes], spread)
                ids = jnp.broadcast_to(sin[p, k:k + 1, 0:1], spread_out.shape)
                rx[pl.ds(p * rows + k * seg_rows, seg_rows), :] = jnp.where(
                    ids == col_slot, spread_out, 0.0
                ).astype(BF16)

    def g_wait():
        for q in x_peers:
            for p in range(NY):
                arrived(g_block(q, p), g_r.at[q, p])

    def product(i):
        place = block(y * NZ + i, chunk)

        total = nn_dot(rx[...], dn[:, :, block(i, chunk)].reshape(slots_wide, chunk))
        for q in range(NX):
            total += nt_dot(gf[q], wn[i, :, q * rows:(q + 1) * rows])
        ot[i] = total.astype(BF16)

        for k, p in enumerate(y_peers):
            copy(ot.at[i, block(p, rows)], out.at[:, place], o_s.at[k, i], o_r.at[y, i], at(y_=p)).start()
        out[:, place] = ot[i, block(y, rows), :]

    def product_step(t):
        for side, i in enumerate((z - t, z + t) if t else (z,)):
            @pl.when(i >= 0 if side == 0 else i < NZ)
            def _():
                if t == NZ - 1:
                    for p in range(NP):
                        arrived(w_piece(i, p), w_r.at[i, p])
                product(i)

    def product0():
        product_step(0)

    def product1():
        product_step(1)

    def product2():
        product_step(2)

    def product3():
        product_step(3)
        for i in range(NZ):
            for k in range(3):
                started.append((who[0], None, lambda: ot.at[0, block(0, rows)], (o_s, k, i)))

    def out_end():
        for p in y_peers:
            for i in range(NZ):
                arrived(out.at[:, block(p * NZ + i, chunk)], o_r.at[p, i])

    def w_step1():
        w_step(1)

    def w_step2():
        w_step(2)

    on(None, slots_out, up_out, w_shift, g_shift)
    on(0, far0, w_start)
    on(None, down_out)
    on(None, picks, up_pick)
    on(0, g_start_y, far1)
    on(None, rank_part)
    on(0, g_start_x)
    on(None, rank_sum, down_part, slots_next_out)
    on(0, g_relay)
    on(1, w_start)
    on(0, w_step1, far2)
    on(1, g_start_y, g_start_x)
    on(None, down_wait)
    on(None, down_pick)
    on(1, down_next)
    on(1, w_step1)
    on(0, w_step2)
    on(1, g_relay)
    on(None, down_sum)
    on(1, dn_start, w_step2)
    on(None, down_hop1, hidden_part)
    on(1, dn_relay)
    on(0, rank_spread, dn_wait0, g_wait, product0, product1, product2)
    on(None, down_hop2, up_part)
    on(1, rank_spread, dn_wait1, g_wait)
    on(0, product3)
    on(1, product0, product1, product2, product3)
    on(None, up_sum, down_end, up_end, out_end)

    for core in (None, 0, 1):
        group = [e[1:] for e in started if e[0] == core]

        def finish():
            for when, like, ss in group:
                def wait():
                    sent(like() if callable(like) else like, ss[0].at[ss[1:]])

                if when is None:
                    wait()
                else:
                    pl.when(when())(wait)

        on(core, finish)


def body(
    activations,
    value_gradient,
    value_matrix,
    adapter_down_weight,
    adapter_up_weight,
    segment_adapter,
    adapter_slot,
):
    rows, width = activations.shape[1:]
    values = value_gradient.shape[2]
    w_rows, v_width = value_matrix.shape[1:]
    rank = adapter_down_weight.shape[2]
    slots = adapter_slot.shape[0]
    piece = width // NY
    vmem = pl.BlockSpec(memory_space=pltpu.VMEM)
    hbm = pl.BlockSpec(memory_space=pltpu.HBM)
    smem = pl.BlockSpec(memory_space=pltpu.SMEM)
    dma = lambda *shape: pltpu.SemaphoreType.DMA(shape)
    scratch = [
        pltpu.VMEM((rows, width), BF16),
        pltpu.VMEM((rows, values), BF16),
        pltpu.VMEM((NZ, w_rows, v_width), BF16),
        pltpu.VMEM((NX, NY * rows, values), BF16),
        pltpu.VMEM((rank, width), BF16),
        pltpu.VMEM((2, rank, width), BF16),
        pltpu.VMEM((NZ, NY * rank, piece), BF16),
        pltpu.VMEM((NY, 8, 128), jnp.int32),
        pltpu.VMEM((NY, 8, 128), jnp.int32),
        pltpu.VMEM((NZ, rank, values), BF16),
        pltpu.VMEM((NY * 2 * rank, values), BF16),
        pltpu.VMEM((NY, 2 * rank, values), BF16),
        pltpu.VMEM((NZ, rank, width), BF16),
        pltpu.VMEM((NY * 2 * rank, width), BF16),
        pltpu.VMEM((NY, 2 * rank, width), BF16),
        pltpu.VMEM((NY * 2 * rank, NZ * rank), BF16),
        pltpu.VMEM((NX, rank, rows), F32),
        pltpu.VMEM((rank, rows), BF16),
        pltpu.VMEM((NY, rank, rows), BF16),
        pltpu.VMEM((NY * rows, slots * rank), BF16),
        pltpu.VMEM((NX, rank, rows), F32),
        pltpu.VMEM((rank, rows), BF16),
        pltpu.VMEM((NY, 2 * rank, width), BF16),
        pltpu.VMEM((NZ, rank, width), BF16),
        pltpu.VMEM((2, NZ, rank, width), BF16),
        pltpu.VMEM((NY, 2 * rank, values), BF16),
        pltpu.VMEM((NZ * rank, values), BF16),
        pltpu.VMEM((NZ, rank, values), BF16),
        pltpu.VMEM((NZ, NY * rows, w_rows), BF16),
        dma(4), dma(NP + 1), dma(NZ, NP), dma(2, NZ, NP),
        dma(NX, NY), dma(3), dma(3, NY), dma(2), dma(3),
        pltpu.SemaphoreType.DMA, dma(NY), dma(NY + 3), dma(NZ), dma(3),
        dma(NY), dma(3), dma(NY), dma(NY),
        dma(NZ), dma(3), dma(NY), dma(3),
        dma(NZ), dma(3), dma(NY), dma(3),
        dma(NX), dma(3), dma(NY), dma(NY),
        dma(NX), dma(3), dma(NY), dma(3), dma(2, NZ), dma(2, NZ),
        dma(NY), dma(3), dma(NZ), dma(3),
        dma(NY, NZ), dma(3, NZ),
    ]
    inputs = [
        pltpu.with_memory_space_constraint(a, pltpu.HBM)
        for a in (
            activations[0], value_gradient[0], value_matrix[0], adapter_down_weight[0, 0], adapter_up_weight[0, 0]
        )
    ]
    received, down_gradient, up_gradient = pl.pallas_call(
        kernel,
        out_shape=(
            jax.ShapeDtypeStruct((rows, width), BF16),
            jax.ShapeDtypeStruct((rank, width), BF16),
            jax.ShapeDtypeStruct((rank, values), BF16),
        ),
        in_specs=[hbm] * 5 + [smem] * 2,
        out_specs=(vmem, vmem, vmem),
        scratch_shapes=scratch,
        compiler_params=pltpu.CompilerParams(
            collective_id=0, has_side_effects=True, vmem_limit_bytes=40 << 20
        ),
        name="relay_backward",
    )(
        *inputs,
        segment_adapter[0],
        adapter_slot,
    )
    return received[None], down_gradient[None, None], up_gradient[None, None]


def solution(mesh):
    placed = (
        P("section", "dp", "mp"),
        P("section", "dp", "mp"),
        P("section", ("mp", "dp"), None),
        P("section", "dp", None, "mp"),
        P("section", "dp", None, "mp"),
        P("section", "dp"),
        P(),
    )
    return jax.shard_map(
        body,
        mesh=mesh,
        in_specs=placed,
        out_specs=(
            P("section", "dp", "mp"),
            P("section", "dp", None, "mp"),
            P("section", "dp", None, "mp"),
        ),
        check_vma=False,
    )
```
